512 devices in a mesh: group: 8 (over z), dom: 64 (over x, y, core).
Axes of the slice: x: 4, y: 8, z: 8, core: 2. Of those that a mesh axis runs over, the one named last changes fastest.
Arguments:
- basis_start: bfloat16 [8, 2304, 32, 128], P('group', 'dom'), may hold values from -4096 to 4096, as said below
- templates: bfloat16 [64, 128, 128], replicated, may hold values from -0.1875 to 0.1875
- template_ids: int32 [8, 2304, 7], P('group', 'dom'), may hold values from 0 to 63
- live_columns: int32 [64], P('dom'), may hold values from 4 to 36, as said below
- face_refs: int32 [2304, 4], P('dom'), may hold values from -1 to 83, as said below
- send_lists: int32 [64, 8, 6], P('dom'), may hold values from -1 to 35, as said below
Outputs:
- basis_q: bfloat16 [8, 2304, 96, 128], P('group', 'dom')
- r_factor: float32 [96, 96], replicated
The draws below stay inside these ranges and needn't reach their ends.
Inputs may be any that keep to these rules, and one draw needn't show every extreme that they name: `basis_start`: standard deviations vary by element, by right-hand side and by slab and piece. Piece d's live columns are slots 0 to live_columns[d] - 1; the pieces and all lists are the same for every slab. `face_refs`: every entry of a live column is -1 (no neighbour) or a slot of the piece's own 36 columns followed by 8 blocks of 6 received slots; own slots are live, received slots are filled ones of the source piece's list. Rows of slots that are not live are -1. `send_lists`: row (d, k) lists live columns of piece d in rising order, then -1; rows toward a position off the grid of pieces are all -1; some row is full.
All inputs are finite; a program needn't handle non-finite values.
Results may differ from the reference program's by a relative error of at most 0.014.
Values may be sent and summed in bfloat16 or wider, within the bound.
A program may use at most 64 MiB of HBM per device.

```python
import math
import jax
import jax.numpy as jnp
from jax import lax

DOF = 128
RHS = 32
TEMPLATES = 64
BLOCK = 4
ZCELLS = 8
COLUMNS = 2304
N_GROUP = 8
N_DOM = 64


DIRECTIONS = ((-1, -1), (-1, 0), (-1, 1), (0, -1), (0, 1), (1, -1), (1, 0), (1, 1))


FACE_STEPS = ((-1, 0), (1, 0), (0, -1), (0, 1))


def partition_layout(key):
    grid_side = math.isqrt(N_DOM)
    grid_cells = BLOCK * grid_side
    column_cap = (BLOCK + 2) * (BLOCK + 2)
    halo_cap = BLOCK + 2
    keys = jax.random.split(jax.random.fold_in(key, 7), 4)
    inner = jnp.arange(1, grid_side, dtype=jnp.int32)
    jitter_rows = jax.random.randint(keys[0], (grid_side - 1,), -1, 2, dtype=jnp.int32)
    chosen_row = jax.random.randint(keys[1], (), 1, grid_side - 1, dtype=jnp.int32)
    jitter_rows = jnp.where(inner == chosen_row, -1, jnp.where(inner == chosen_row + 1, 1, jitter_rows))
    row_cuts = jnp.concatenate([jnp.zeros((1,), jnp.int32), BLOCK * inner + jitter_rows, jnp.full((1,), grid_cells, jnp.int32)])
    jitter_cols = jax.random.randint(keys[2], (grid_side, grid_side - 1), -1, 2, dtype=jnp.int32)
    chosen_col = jax.random.randint(keys[3], (), 1, grid_side - 1, dtype=jnp.int32)
    picked = jnp.arange(grid_side, dtype=jnp.int32)[:, None] == chosen_row
    jitter_cols = jnp.where(picked & (inner[None, :] == chosen_col), -1, jnp.where(picked & (inner[None, :] == chosen_col + 1), 1, jitter_cols))
    column_cuts = jnp.concatenate([jnp.zeros((grid_side, 1), jnp.int32), BLOCK * inner[None, :] + jitter_cols, jnp.full((grid_side, 1), grid_cells, jnp.int32)], 1)
    heights = row_cuts[1:] - row_cuts[:-1]
    widths = column_cuts[:, 1:] - column_cuts[:, :-1]
    pieces = jnp.arange(N_DOM, dtype=jnp.int32)
    piece_row = pieces // grid_side
    piece_col = pieces % grid_side
    counts = heights[piece_row] * widths[piece_row, piece_col]
    slots = jnp.arange(column_cap, dtype=jnp.int32)
    piece_width = widths[piece_row, piece_col][:, None]
    live_mask = slots[None, :] < counts[:, None]
    cell_x = row_cuts[piece_row][:, None] + slots[None, :] // piece_width
    cell_y = column_cuts[piece_row, piece_col][:, None] + slots[None, :] % piece_width
    face_x = cell_x[:, :, None] + jnp.array([f[0] for f in FACE_STEPS], jnp.int32)
    face_y = cell_y[:, :, None] + jnp.array([f[1] for f in FACE_STEPS], jnp.int32)
    inside = (face_x >= 0) & (face_x < grid_cells) & (face_y >= 0) & (face_y < grid_cells)
    clip_x = jnp.clip(face_x, 0, grid_cells - 1)
    clip_y = jnp.clip(face_y, 0, grid_cells - 1)
    owner_row = jnp.sum((clip_x[..., None] >= row_cuts[1:grid_side]).astype(jnp.int32), -1)
    owner_col = jnp.sum((clip_y[..., None] >= column_cuts[owner_row][..., 1:grid_side]).astype(jnp.int32), -1)
    owner = owner_row * grid_side + owner_col
    owner_slot = (clip_x - row_cuts[owner_row]) * widths[owner_row, owner_col] + clip_y - column_cuts[owner_row, owner_col]
    step_x = jnp.array([d[0] for d in DIRECTIONS], jnp.int32)
    step_y = jnp.array([d[1] for d in DIRECTIONS], jnp.int32)
    target_row = piece_row[:, None] + step_x[None, :]
    target_col = piece_col[:, None] + step_y[None, :]
    target_ok = (target_row >= 0) & (target_row < grid_side) & (target_col >= 0) & (target_col < grid_side)
    target = target_row * grid_side + target_col
    touching = jnp.any(inside[:, None] & (owner[:, None] == target[:, :, None, None]), -1)
    flags = live_mask[:, None, :] & target_ok[:, :, None] & touching
    ranks = jnp.cumsum(flags.astype(jnp.int32), 2) - 1
    places = jnp.arange(halo_cap, dtype=jnp.int32)
    hits = flags[:, :, None, :] & (ranks[:, :, None, :] == places[None, None, :, None])
    send_lists = jnp.where(jnp.any(hits, -1), jnp.sum(jnp.where(hits, slots, 0), -1), -1).astype(jnp.int32)
    same_piece = owner == pieces[:, None, None]
    dir_x = piece_row[:, None, None] - owner_row
    dir_y = piece_col[:, None, None] - owner_col
    matches = (dir_x[..., None] == step_x) & (dir_y[..., None] == step_y)
    which = jnp.sum(jnp.arange(8, dtype=jnp.int32) * matches.astype(jnp.int32), -1)
    ghost_rank = ranks[owner, which, owner_slot]
    refs = jnp.where(live_mask[:, :, None] & inside, jnp.where(same_piece, owner_slot, column_cap + which * halo_cap + ghost_rank), -1)
    return (counts.astype(jnp.int32), refs.reshape(N_DOM * column_cap, 4).astype(jnp.int32), send_lists)


def draw_live_columns(key, part):
    return partition_layout(key)[0]


def draw_face_refs(key, part):
    return partition_layout(key)[1]


def draw_send_lists(key, part):
    return partition_layout(key)[2]


def draw_basis_start(key, part):
    key = jax.random.fold_in(key, 11)
    keys = jax.random.split(key, 6)
    shape = (ZCELLS, COLUMNS, RHS, DOF)
    element_scale = jnp.exp(jax.random.uniform(keys[0], (ZCELLS, COLUMNS, 1, 1), jnp.float32, 0.0, math.log(10.0)))
    rhs_scale = jnp.exp(jax.random.uniform(keys[1], (1, 1, RHS, 1), jnp.float32, 0.0, math.log(10.0)))
    device_scale = jnp.exp(jax.random.uniform(keys[4], (N_GROUP, N_DOM), jnp.float32, 0.0, math.log(3.0)))
    heavy_device = jax.random.randint(keys[5], (), 0, N_GROUP * N_DOM, dtype=jnp.int32)
    device_index = jnp.arange(N_GROUP * N_DOM, dtype=jnp.int32).reshape(N_GROUP, N_DOM)
    device_scale = jnp.where(device_index == heavy_device, 16.0 * device_scale, device_scale)
    piece_scale = jnp.repeat(jnp.repeat(device_scale, ZCELLS // N_GROUP, 0), COLUMNS // N_DOM, 1)[:, :, None, None]
    base = jnp.clip(jax.random.normal(keys[2], shape, jnp.float32), -6.0, 6.0)
    values = base * element_scale * rhs_scale * piece_scale * 0.1
    return values.astype(jnp.bfloat16)


def set_ends(values, stream_key, least, top_value):
    longest = values.shape.index(max(values.shape))
    spots = []
    for shift in (0, 1):
        where = [jax.random.randint(jax.random.fold_in(stream_key, axis), (), 0, length) for axis, length in enumerate(values.shape)]
        where[longest] = (where[longest] + shift) % values.shape[longest]
        spots.append(tuple(where))
    return values.at[spots[0]].set(least).at[spots[1]].set(top_value)


def scatter_about(key, shape, spread, reach, kind=jnp.bfloat16):
    drawn = spread * jax.random.normal(key, shape, jnp.float32)
    return jnp.clip(drawn, min=-reach, max=reach).astype(kind)


def setup_inputs(seed: int = 0) -> dict:
    key_list = jax.random.split(jax.random.key(seed), 7)
    basis_start = draw_basis_start(jax.random.fold_in(key_list[6], 71), 0)
    templates = scatter_about(key_list[1], (TEMPLATES, DOF, DOF), (7 * DOF) ** -0.5, 0.1875)
    template_ids = set_ends(jax.random.randint(key_list[2], (ZCELLS, COLUMNS, 7), 0, TEMPLATES), jax.random.fold_in(key_list[2], 1), 0, TEMPLATES - 1).astype(jnp.int32)
    live_columns = draw_live_columns(jax.random.fold_in(key_list[6], 71), 0)
    face_refs = draw_face_refs(jax.random.fold_in(key_list[6], 71), 0)
    send_lists = draw_send_lists(jax.random.fold_in(key_list[6], 71), 0)
    return dict(basis_start=basis_start, templates=templates, template_ids=template_ids, live_columns=live_columns, face_refs=face_refs, send_lists=send_lists)


DIRECTIONS = ((-1, -1), (-1, 0), (-1, 1), (0, -1), (0, 1), (1, -1), (1, 0), (1, 1))

def reference(basis_start, templates, template_ids, live_columns, face_refs, send_lists):
    depth_cells, columns, rhs_count, dof_count = basis_start.shape
    piece_count = live_columns.shape[0]
    grid_side = math.isqrt(piece_count)
    column_cap = columns // piece_count
    halo_cap = send_lists.shape[2]
    live_mask = (jnp.arange(column_cap, dtype=jnp.int32)[None, :] < live_columns[:, None]).reshape(columns)
    masked_start = jnp.where(live_mask[None, :, None, None], basis_start, jnp.zeros((), jnp.bfloat16))
    domain_ids = jnp.arange(piece_count, dtype=jnp.int32)
    piece_row = domain_ids // grid_side
    piece_col = domain_ids % grid_side
    step_x = jnp.array([d[0] for d in DIRECTIONS], jnp.int32)
    step_y = jnp.array([d[1] for d in DIRECTIONS], jnp.int32)
    source_row = piece_row[:, None] - step_x[None]
    source_col = piece_col[:, None] - step_y[None]
    inside = (source_row >= 0) & (source_row < grid_side) & (source_col >= 0) & (source_col < grid_side)
    source = jnp.clip(source_row, 0, grid_side - 1) * grid_side + jnp.clip(source_col, 0, grid_side - 1)
    entries = send_lists[source, jnp.arange(8, dtype=jnp.int32)[None, :]]
    ghost_ok = (inside[:, :, None] & (entries >= 0)).reshape(piece_count, 8 * halo_cap)
    ghost_global = (source[:, :, None] * column_cap + jnp.maximum(entries, 0)).reshape(piece_count, 8 * halo_cap)
    neighbour_refs = face_refs.reshape(piece_count, column_cap, 4)
    is_own = neighbour_refs < column_cap
    ghost_slot = jnp.clip(neighbour_refs - column_cap, 0, 8 * halo_cap - 1)
    through = ghost_global[domain_ids[:, None, None], ghost_slot]
    through_ok = ghost_ok[domain_ids[:, None, None], ghost_slot]
    target = jnp.where(is_own, domain_ids[:, None, None] * column_cap + jnp.maximum(neighbour_refs, 0), through).reshape(columns, 4)
    valid_ref = ((neighbour_refs >= 0) & jnp.where(is_own, True, through_ok)).reshape(columns, 4)
    zero_block = jnp.zeros((columns, rhs_count, dof_count), jnp.bfloat16)

    def operate(vector):

        def one_layer(depth):
            centre = vector[depth]
            below_part = jnp.where(depth > 0, vector[jnp.maximum(depth - 1, 0)], zero_block)
            above_part = jnp.where(depth < depth_cells - 1, vector[jnp.minimum(depth + 1, depth_cells - 1)], zero_block)
            beside = jnp.where(valid_ref[:, :, None, None], centre[target], jnp.zeros((), jnp.bfloat16))
            operands = jnp.concatenate([jnp.stack([centre, below_part, above_part], 1), beside], 1)
            operands = operands.reshape(piece_count, column_cap, 7, rhs_count, dof_count)
            layer_ids = template_ids[depth].reshape(piece_count, column_cap, 7)

            def device_block(pair):
                block_ops, block_ids = pair
                weights = templates[block_ids].astype(jnp.float32)
                return jnp.einsum('cfij,cfrj->cri', weights, block_ops.astype(jnp.float32))
            result = lax.map(device_block, (operands, layer_ids))
            return result.reshape(columns, rhs_count, dof_count)
        return lax.map(one_layer, jnp.arange(depth_cells, dtype=jnp.int32))
    first_power = operate(masked_start).astype(jnp.bfloat16)
    second_power = operate(first_power).astype(jnp.bfloat16)

    def stacked_at(depth):
        return jnp.concatenate([masked_start[depth], first_power[depth], second_power[depth]], 1).astype(jnp.float32)

    def gram_term(depth):
        block = stacked_at(depth)
        return jnp.einsum('cpd,cqd->pq', block, block)
    gram_matrix = lax.optimization_barrier(jnp.sum(lax.map(gram_term, jnp.arange(depth_cells, dtype=jnp.int32)), 0))
    gram_matrix = gram_matrix / (depth_cells * columns * dof_count)
    lower_factor = jnp.linalg.cholesky(gram_matrix)
    basis_width = gram_matrix.shape[0]
    inverse = lax.linalg.triangular_solve(lower_factor, jnp.eye(basis_width, dtype=gram_matrix.dtype), left_side=True, lower=True)

    def project(depth):
        return jnp.einsum('cpd,qp->cqd', stacked_at(depth), inverse, precision=lax.Precision.HIGHEST).astype(jnp.bfloat16)
    basis_q = lax.map(project, jnp.arange(depth_cells, dtype=jnp.int32))
    return (basis_q, lower_factor.T)
```

```python
import functools
import math

import jax
import jax.numpy as jnp
from jax import lax
from jax.experimental import pallas as pl
from jax.experimental.pallas import tpu as pltpu
from jax.sharding import PartitionSpec as P

DIRECTIONS = ((-1, -1), (-1, 0), (-1, 1), (0, -1), (0, 1), (1, -1), (1, 0), (1, 1))
MESH = pl.DeviceIdType.MESH
F32 = jnp.float32
BF16 = jnp.bfloat16
NT = (((1,), (1,)), ((), ()))
HIGH = lax.Precision.HIGHEST


def dot(x, y):
    return jnp.dot(x, y, preferred_element_type=F32)


def dot_nt(x, y):
    return lax.dot_general(x, y, NT, preferred_element_type=F32)


def exact(x, y):
    return jnp.dot(x, y, preferred_element_type=F32, precision=HIGH)


def exact_nt(x, y):
    return lax.dot_general(x, y, NT, preferred_element_type=F32, precision=HIGH)


def kernel(
    groups, side, peers_y, rows_total,
    basis_ref, templates_ref, ids_ref, live_ref, refs_ref, lists_ref,
    q_ref, r_ref,
    tmpl, v0, v1, v2, ghost1, ghost2, packet1, packet2, layer1, layer2, acc,
    part, part_in, mid, mid_in, far, far_in, done, work, upper, inv,
    load_sem, halo_send, halo_recv, sum_send, sum_recv,
):
    column_cap, rhs, dof = v0.shape[0] - 1, v0.shape[1], v0.shape[2]
    halo_cap = packet1.shape[1]
    zero_own, zero_ghost = column_cap, 8 * halo_cap
    vectors, ghosts, layers = (v0, v1, v2), (ghost1, ghost2), (layer1, layer2)
    packets = (packet1, packet2)
    pieces = side * side
    peers_x = pieces // peers_y
    g = lax.axis_index("group")
    d = lax.axis_index("dom")
    row, col = d // side, d % side
    core, at_y, at_x = d % 2, (d // 2) % peers_y, d // (2 * peers_y)
    me_x = at_x * 2 + core

    def on_z(offset):
        return ((g + offset) % groups, d)

    def on_y(offset):
        return (g, (at_x * peers_y + (at_y + offset) % peers_y) * 2 + core)

    def on_x(offset):
        other = (me_x + offset) % peers_x
        return (g, ((other // 2) * peers_y + at_y) * 2 + other % 2)

    def inside(dx, dy):
        return (row + dx >= 0) & (row + dx < side) & (col + dy >= 0) & (col + dy < side)

    load_templates = pltpu.make_async_copy(templates_ref, tmpl, load_sem.at[0])
    load_templates.start()
    load_basis = pltpu.make_async_copy(basis_ref.at[0], v0.at[pl.ds(0, column_cap)], load_sem.at[1])
    load_basis.start()

    barrier = pltpu.get_barrier_semaphore()

    def greet(device):
        pl.semaphore_signal(barrier, inc=1, device_id=device, device_id_type=MESH)

    expected = 0
    for dx, dy in DIRECTIONS:
        target = (g, (row + dx) * side + col + dy)
        pl.when(inside(dx, dy))(functools.partial(greet, target))
        expected += inside(dx, dy).astype(jnp.int32)
    for peers, place in ((groups, on_z), (peers_y, on_y), (peers_x, on_x)):
        for offset in range(1, peers):
            greet(place(offset))
        expected += peers - 1

    empty = jnp.zeros((rhs, dof), BF16)
    for vector in vectors:
        vector[zero_own] = empty
    for x in range(2):
        ghosts[x][zero_ghost] = empty
        for k, (dx, dy) in enumerate(DIRECTIONS):
            @pl.when(jnp.logical_not(inside(-dx, -dy)))
            def _():
                ghosts[x][pl.ds(k * halo_cap, halo_cap)] = jnp.zeros((halo_cap, rhs, dof), BF16)

        @pl.when(g == 0)
        def _():
            layers[x][0] = jnp.zeros((column_cap, rhs, dof), BF16)

        @pl.when(g == groups - 1)
        def _():
            layers[x][1] = jnp.zeros((column_cap, rhs, dof), BF16)

    live = live_ref[0]
    load_basis.wait()

    @pl.loop(0, column_cap)
    def _(c):
        v0[c] = v0[c] * (c < live).astype(F32).astype(BF16)

    pl.semaphore_wait(barrier, expected)

    def plane_copy(x, k):
        dx, dy = DIRECTIONS[k]
        return pltpu.make_async_remote_copy(
            src_ref=packets[x].at[k],
            dst_ref=ghosts[x].at[pl.ds(k * halo_cap, halo_cap)],
            send_sem=halo_send.at[x, k],
            recv_sem=halo_recv.at[x, k],
            device_id=(g, (row + dx) * side + col + dy),
            device_id_type=MESH,
        )

    def layer_copy(x, up):
        return pltpu.make_async_remote_copy(
            src_ref=vectors[x].at[pl.ds(0, column_cap)],
            dst_ref=layers[x].at[0 if up else 1],
            send_sem=halo_send.at[x, 8 + up],
            recv_sem=halo_recv.at[x, 8 + up],
            device_id=(g + 1 if up else g - 1, d),
            device_id_type=MESH,
        )

    has_up, has_down = g < groups - 1, g > 0
    order = (6, 1, 5, 7, 0, 2, 3, 4)

    def halo_start(x):
        vector = vectors[x]
        for k in order:
            for s in range(halo_cap):
                slot = lists_ref[0, k, s]
                packets[x][k, s] = vector[jnp.where(slot < 0, zero_own, slot)]
            pl.when(inside(*DIRECTIONS[k]))(lambda: plane_copy(x, k).start())
        pl.when(has_up)(lambda: layer_copy(x, 1).start())
        pl.when(has_down)(lambda: layer_copy(x, 0).start())

    def layers_wait(x):
        pl.when(has_down)(lambda: layer_copy(x, 1).wait_recv())
        pl.when(has_up)(lambda: layer_copy(x, 0).wait_recv())

    def plane_wait(x):
        for k in order:
            dx, dy = DIRECTIONS[k]
            pl.when(inside(-dx, -dy))(lambda: plane_copy(x, k).wait_recv())

    def halo_sent(x):
        for k in order:
            pl.when(inside(*DIRECTIONS[k]))(lambda: plane_copy(x, k).wait_send())
        pl.when(has_up)(lambda: layer_copy(x, 1).wait_send())
        pl.when(has_down)(lambda: layer_copy(x, 0).wait_send())

    def apply(blocks, c, faces):
        weights = jnp.concatenate([tmpl[ids_ref[0, c, f]] for f in faces], axis=1)
        return dot_nt(jnp.concatenate(blocks, axis=1), weights)

    def own_pass(x):
        vector = vectors[x]

        @pl.loop(0, column_cap)
        def _(c):
            blocks = [vector[c]]
            for q in range(4):
                r = refs_ref[c, q]
                blocks.append(vector[jnp.where((r < 0) | (r >= column_cap), zero_own, r)])
            acc[c] = apply(blocks, c, (0, 3, 4, 5, 6))

    def layer_pass(x):
        @pl.loop(0, column_cap)
        def _(c):
            acc[c] = acc[c] + apply([layers[x][0, c], layers[x][1, c]], c, (1, 2))

    def ghost_pass(x):
        @pl.loop(0, column_cap)
        def _(c):
            blocks = []
            for q in range(4):
                r = refs_ref[c, q]
                blocks.append(ghosts[x][jnp.where(r < column_cap, zero_ghost, r - column_cap)])
            total = acc[c] + apply(blocks, c, (3, 4, 5, 6))
            vectors[x + 1][c] = jnp.where(c < live, total, 0.0).astype(BF16)

    def gram_rows(j):
        @functools.partial(lax.fori_loop, 0, column_cap // 2, init_val=jnp.zeros((rhs, rhs * (j + 1)), F32))
        def total(h, carry):
            pair = [
                jnp.concatenate([vectors[i][2 * h], vectors[i][2 * h + 1]], axis=1)
                for i in range(j + 1)
            ]
            return carry + dot_nt(pair[j], jnp.concatenate(pair, axis=0))

        work[:, : rhs * (j + 1)] = total

    share = rhs // groups

    def send_all(j, phase, peers, place, source, slots, at):
        copies = []
        for offset in range(1, peers):
            copies.append(pltpu.make_async_remote_copy(
                src_ref=source(offset),
                dst_ref=slots.at[j, at],
                send_sem=sum_send.at[j, phase, offset],
                recv_sem=sum_recv.at[j, phase, offset],
                device_id=place(offset),
                device_id_type=MESH,
            ))
        for copy in copies:
            copy.start()
        return copies

    def add_up(slots, j, peers):
        total = slots[j, 0]
        for s in range(1, peers):
            total = total + slots[j, s]
        return total

    def reduce_steps(j):
        for s in range(groups):
            part[j, s] = work[s * share : (s + 1) * share, :]
        part_in[j, g] = part[j, g]
        copies = send_all(j, 0, groups, on_z, lambda o: part.at[j, (g + o) % groups], part_in, g)
        yield
        for copy in copies:
            copy.wait()
        mid[j] = add_up(part_in, j, groups)
        mid_in[j, at_y] = mid[j]
        copies = send_all(j, 1, peers_y, on_y, lambda o: mid.at[j], mid_in, at_y)
        yield
        for copy in copies:
            copy.wait()
        far[j] = add_up(mid_in, j, peers_y)
        far_in[j, me_x] = far[j]
        copies = send_all(j, 2, peers_x, on_x, lambda o: far.at[j], far_in, me_x)
        yield
        for copy in copies:
            copy.wait()
        done[j, g] = add_up(far_in, j, peers_x)
        copies = send_all(j, 3, groups, on_z, lambda o: done.at[j, g], done, g)
        yield
        for copy in copies:
            copy.wait()
        for s in range(groups):
            work[s * share : (s + 1) * share, :] = done[j, s] * (1.0 / rows_total)
        yield

    lanes = work.shape[1]
    wide = lax.broadcasted_iota(jnp.int32, (rhs, lanes), 1)
    tall = lax.broadcasted_iota(jnp.int32, (rhs, lanes), 0)

    def factor(j):
        before = rhs * j
        corner = work[:, before : before + rhs]
        if j:
            left = exact_nt(work[:, :before], inv[:before, :before])
            corner = corner - exact_nt(left, left)
        work[...] = jnp.where(wide == tall + rhs, 1.0, 0.0)
        work[:, :rhs] = corner
        m = work[...]
        for p in range(rhs // 8):
            size = rhs - 8 * p
            cols = [jnp.broadcast_to(m[:, 8 * p + i : 8 * p + i + 1], (size, lanes)) for i in range(8)]
            for i in range(8):
                scale = lax.rsqrt(jnp.broadcast_to(cols[i][i : i + 1, :], (size, lanes)))
                column = cols[i] * scale
                line = jnp.broadcast_to(m[i : i + 1, :], (size, lanes)) * scale
                upper[8 * p + i : 8 * p + i + 1, :] = line[0:1, :]
                m = m - column * line
                for n in range(i + 1, 8):
                    cols[n] = cols[n] - column * jnp.broadcast_to(column[n : n + 1, :], (size, lanes))
            m = m[8:]
        square = lax.broadcasted_iota(jnp.int32, (rhs, rhs), 0)
        across = lax.broadcasted_iota(jnp.int32, (rhs, rhs), 1)
        r_ref[before : before + rhs, before : before + rhs] = jnp.where(
            across >= square, upper[:, :rhs], 0.0
        )
        corner_inv = upper[:, rhs : 2 * rhs]
        inv[before : before + rhs, before : before + rhs] = corner_inv
        if j:
            r_ref[:before, before : before + rhs] = left.T
            r_ref[before : before + rhs, :before] = jnp.zeros((rhs, before), F32)
            inv[before : before + rhs, :before] = -exact(corner_inv, exact(left, inv[:before, :before]))

    def project(j):
        width = rhs * (j + 1)
        rows = inv[rhs * j : width, :width]
        high = rows.astype(BF16)
        low = (rows - high.astype(F32)).astype(BF16)
        both = jnp.concatenate([high, low], axis=1)

        @pl.loop(0, column_cap)
        def _(c):
            stack = [vectors[i][c] for i in range(j + 1)]
            q_ref[0, c, rhs * j : width, :] = dot(both, jnp.concatenate(stack + stack, axis=0)).astype(BF16)

    halo_start(0)
    gram_rows(0)
    stage = reduce_steps(0)
    next(stage)
    load_templates.wait()
    own_pass(0)
    next(stage)
    layers_wait(0)
    layer_pass(0)
    next(stage)
    next(stage)
    plane_wait(0)
    ghost_pass(0)

    halo_start(1)
    next(stage)
    factor(0)
    project(0)
    gram_rows(1)
    stage = reduce_steps(1)
    next(stage)
    own_pass(1)
    next(stage)
    layers_wait(1)
    layer_pass(1)
    next(stage)
    next(stage)
    next(stage)
    factor(1)
    project(1)
    plane_wait(1)
    ghost_pass(1)

    gram_rows(2)
    for _ in reduce_steps(2):
        pass
    factor(2)
    project(2)
    halo_sent(0)
    halo_sent(1)


def solution(mesh):
    groups, pieces = mesh.shape["group"], mesh.shape["dom"]
    side = math.isqrt(pieces)
    peers_y = min(8, pieces // 2)
    peers_x = pieces // peers_y

    def body(basis_start, templates, template_ids, live_columns, face_refs, send_lists):
        _, column_cap, rhs, dof = basis_start.shape
        halo_cap = send_lists.shape[2]
        width = 3 * rhs
        share = rhs // groups
        lanes = 128
        rows_total = column_cap * dof * groups * pieces
        vmem, smem = pltpu.VMEM, pltpu.SMEM
        block = (rhs, dof)
        return pl.pallas_call(
            functools.partial(kernel, groups, side, peers_y, rows_total),
            out_shape=(
                jax.ShapeDtypeStruct((1, column_cap, width, dof), BF16),
                jax.ShapeDtypeStruct((width, width), F32),
            ),
            in_specs=[pl.BlockSpec(memory_space=pl.ANY)] * 2 + [pl.BlockSpec(memory_space=smem)] * 4,
            out_specs=(pl.BlockSpec(memory_space=vmem), pl.BlockSpec(memory_space=vmem)),
            scratch_shapes=[
                vmem(templates.shape, BF16),
                vmem((column_cap + 1, *block), BF16),
                vmem((column_cap + 1, *block), BF16),
                vmem((column_cap + 1, *block), BF16),
                vmem((8 * halo_cap + 1, *block), BF16),
                vmem((8 * halo_cap + 1, *block), BF16),
                vmem((8, halo_cap, *block), BF16),
                vmem((8, halo_cap, *block), BF16),
                vmem((2, column_cap, *block), BF16),
                vmem((2, column_cap, *block), BF16),
                vmem((column_cap, *block), F32),
                vmem((3, groups, share, lanes), F32),
                vmem((3, groups, share, lanes), F32),
                vmem((3, share, lanes), F32),
                vmem((3, peers_y, share, lanes), F32),
                vmem((3, share, lanes), F32),
                vmem((3, peers_x, share, lanes), F32),
                vmem((3, groups, share, lanes), F32),
                vmem((rhs, lanes), F32),
                vmem((rhs, lanes), F32),
                vmem((width, lanes), F32),
                pltpu.SemaphoreType.DMA((2,)),
                pltpu.SemaphoreType.DMA((2, 10)),
                pltpu.SemaphoreType.DMA((2, 10)),
                pltpu.SemaphoreType.DMA((3, 4, 8)),
                pltpu.SemaphoreType.DMA((3, 4, 8)),
            ],
            compiler_params=pltpu.CompilerParams(
                collective_id=0, has_side_effects=True, vmem_limit_bytes=40 * 2**20
            ),
        )(basis_start, templates, template_ids, live_columns, face_refs, send_lists)

    return jax.shard_map(
        body,
        mesh=mesh,
        in_specs=(
            P("group", "dom", None, None),
            P(),
            P("group", "dom", None),
            P("dom"),
            P("dom", None),
            P("dom", None, None),
        ),
        out_specs=(P("group", "dom", None, None), P()),
        check_vma=False,
    )
```

```python
import functools
import math

import jax
import jax.numpy as jnp
from jax import lax
from jax.experimental import pallas as pl
from jax.experimental.pallas import tpu as pltpu
from jax.sharding import PartitionSpec as P

DIRECTIONS = ((-1, -1), (-1, 0), (-1, 1), (0, -1), (0, 1), (1, -1), (1, 0), (1, 1))
MESH = pl.DeviceIdType.MESH
F32 = jnp.float32
BF16 = jnp.bfloat16
NT = (((1,), (1,)), ((), ()))
HIGH = lax.Precision.HIGHEST
UN_OWN = UN_LAYER = UN_GHOST = UN_PROJ = 12
UN_GRAM = 9


def dot(x, y):
    return jnp.dot(x, y, preferred_element_type=F32)


def dot_nt(x, y):
    return lax.dot_general(x, y, NT, preferred_element_type=F32)


def exact(x, y):
    return jnp.dot(x, y, preferred_element_type=F32, precision=HIGH)


def exact_nt(x, y):
    return lax.dot_general(x, y, NT, preferred_element_type=F32, precision=HIGH)


def kernel(
    groups, side, peers_y, rows_total,
    basis_ref, templates_ref, ids_ref, live_ref, refs_ref, lists_ref,
    q_ref, r_ref,
    tmpl, v0, v1, v2, ghost1, ghost2, packet1, packet2, layer1, layer2, acc,
    slots_a, slots_b, work, upper, inv,
    load_sem, halo_send, halo_recv, sum_send, sum_recv,
):
    column_cap, rhs, dof = v0.shape[0] - 1, v0.shape[1], v0.shape[2]
    halo_cap = packet1.shape[1]
    zero_own, zero_ghost = column_cap, 8 * halo_cap
    vectors, ghosts, layers = (v0, v1, v2), (ghost1, ghost2), (layer1, layer2)
    packets = (packet1, packet2)
    pieces = side * side
    peers_x = pieces // peers_y
    g = lax.axis_index("group")
    d = lax.axis_index("dom")
    row, col = d // side, d % side
    core, at_y, at_x = d % 2, (d // 2) % peers_y, d // (2 * peers_y)
    me_x = at_x * 2 + core

    def on_z(offset):
        return ((g + offset) % groups, d)

    def on_y(offset):
        return (g, (at_x * peers_y + (at_y + offset) % peers_y) * 2 + core)

    def on_x(offset):
        other = (me_x + offset) % peers_x
        return (g, ((other // 2) * peers_y + at_y) * 2 + other % 2)

    def inside(dx, dy):
        return (row + dx >= 0) & (row + dx < side) & (col + dy >= 0) & (col + dy < side)

    load_templates = pltpu.make_async_copy(templates_ref, tmpl, load_sem.at[0])
    load_templates.start()
    load_basis = pltpu.make_async_copy(basis_ref.at[0], v0.at[pl.ds(0, column_cap)], load_sem.at[1])
    load_basis.start()

    barrier = pltpu.get_barrier_semaphore()

    def greet(device):
        pl.semaphore_signal(barrier, inc=1, device_id=device, device_id_type=MESH)

    expected = 0
    for dx, dy in DIRECTIONS:
        target = (g, (row + dx) * side + col + dy)
        pl.when(inside(dx, dy))(functools.partial(greet, target))
        expected += inside(dx, dy).astype(jnp.int32)
    for peers, place in ((groups, on_z), (peers_y, on_y), (peers_x, on_x)):
        for offset in range(1, peers):
            greet(place(offset))
        expected += peers - 1

    empty = jnp.zeros((rhs, dof), BF16)
    for vector in vectors:
        vector[zero_own] = empty
    for x in range(2):
        ghosts[x][zero_ghost] = empty
        for k, (dx, dy) in enumerate(DIRECTIONS):
            @pl.when(jnp.logical_not(inside(-dx, -dy)))
            def _():
                ghosts[x][pl.ds(k * halo_cap, halo_cap)] = jnp.zeros((halo_cap, rhs, dof), BF16)

        @pl.when(g == 0)
        def _():
            layers[x][0] = jnp.zeros((column_cap, rhs, dof), BF16)

        @pl.when(g == groups - 1)
        def _():
            layers[x][1] = jnp.zeros((column_cap, rhs, dof), BF16)

    inv[...] = jnp.zeros(inv.shape, F32)
    live = live_ref[0]
    load_basis.wait()

    @pl.loop(0, column_cap)
    def _(c):
        v0[c] = v0[c] * (c < live).astype(F32).astype(BF16)

    pl.semaphore_wait(barrier, expected)

    def plane_copy(x, k):
        dx, dy = DIRECTIONS[k]
        return pltpu.make_async_remote_copy(
            src_ref=packets[x].at[k],
            dst_ref=ghosts[x].at[pl.ds(k * halo_cap, halo_cap)],
            send_sem=halo_send.at[x, k],
            recv_sem=halo_recv.at[x, k],
            device_id=(g, (row + dx) * side + col + dy),
            device_id_type=MESH,
        )

    def layer_copy(x, up):
        return pltpu.make_async_remote_copy(
            src_ref=vectors[x].at[pl.ds(0, column_cap)],
            dst_ref=layers[x].at[0 if up else 1],
            send_sem=halo_send.at[x, 8 + up],
            recv_sem=halo_recv.at[x, 8 + up],
            device_id=(g + 1 if up else g - 1, d),
            device_id_type=MESH,
        )

    has_up, has_down = g < groups - 1, g > 0
    order = (6, 1, 5, 7, 0, 2, 3, 4)

    def halo_start(x):
        vector = vectors[x]
        for k in order:
            if k == 3:
                pl.when(has_up)(lambda: layer_copy(x, 1).start())
                pl.when(has_down)(lambda: layer_copy(x, 0).start())
            for s in range(halo_cap):
                slot = lists_ref[s, 0, k]
                packets[x][k, s] = vector[jnp.where(slot < 0, zero_own, slot)]
            pl.when(inside(*DIRECTIONS[k]))(lambda: plane_copy(x, k).start())

    def layers_wait(x):
        pl.when(has_down)(lambda: layer_copy(x, 1).wait_recv())
        pl.when(has_up)(lambda: layer_copy(x, 0).wait_recv())

    def plane_wait(x):
        for k in order:
            dx, dy = DIRECTIONS[k]
            pl.when(inside(-dx, -dy))(lambda: plane_copy(x, k).wait_recv())

    def halo_sent(x):
        for k in order:
            pl.when(inside(*DIRECTIONS[k]))(lambda: plane_copy(x, k).wait_send())
        pl.when(has_up)(lambda: layer_copy(x, 1).wait_send())
        pl.when(has_down)(lambda: layer_copy(x, 0).wait_send())

    def apply(blocks, c, faces):
        weights = jnp.concatenate([tmpl[ids_ref[f, 0, c]] for f in faces], axis=0)
        return dot(jnp.concatenate(blocks, axis=1), weights)

    def own_pass(x):
        vector = vectors[x]

        @pl.loop(0, column_cap, unroll=UN_OWN)
        def _(c):
            blocks = [vector[c]]
            for q in range(4):
                r = refs_ref[q, c]
                blocks.append(vector[jnp.where((r < 0) | (r >= column_cap), zero_own, r)])
            acc[c] = apply(blocks, c, (0, 3, 4, 5, 6))

    def layer_pass(x):
        @pl.loop(0, column_cap, unroll=UN_LAYER)
        def _(c):
            acc[c] = acc[c] + apply([layers[x][0, c], layers[x][1, c]], c, (1, 2))

    def ghost_pass(x):
        @pl.loop(0, column_cap, unroll=UN_GHOST)
        def _(c):
            blocks = []
            for q in range(4):
                r = refs_ref[q, c]
                blocks.append(ghosts[x][jnp.where(r < column_cap, zero_ghost, r - column_cap)])
            total = acc[c] + apply(blocks, c, (3, 4, 5, 6))
            vectors[x + 1][c] = jnp.where(c < live, total, 0.0).astype(BF16)

    def gram(rows):
        def add(h, carry):
            pair = [
                jnp.concatenate([vectors[i][2 * h], vectors[i][2 * h + 1]], axis=1)
                for i in range(rows[-1] + 1)
            ]
            return tuple(
                total + dot_nt(pair[j], jnp.concatenate(pair[: j + 1], axis=0))
                for j, total in zip(rows, carry)
            )

        start = tuple(jnp.zeros((rhs, rhs * (j + 1)), F32) for j in rows)
        totals = lax.fori_loop(0, column_cap // 2, add, start, unroll=UN_GRAM)
        return [t[:, rhs * i : rhs * (i + 1)] for t in totals for i in range(t.shape[1] // rhs)]

    def pack(block):
        return jnp.concatenate([block[8 * i : 8 * i + 8] for i in range(rhs // 8)], axis=1)

    def unpack(line):
        return jnp.concatenate([line[:, rhs * i : rhs * (i + 1)] for i in range(rhs // 8)], axis=0)

    def send_all(w, hop, peers, place, source, slots, at):
        copies = [
            pltpu.make_async_remote_copy(
                src_ref=source,
                dst_ref=slots.at[at],
                send_sem=sum_send.at[w, hop, offset],
                recv_sem=sum_recv.at[w, hop, offset],
                device_id=place(offset),
                device_id_type=MESH,
            )
            for offset in range(1, peers)
        ]
        for copy in copies:
            copy.start()
        return copies

    def add_up(slots, peers):
        total = slots[0]
        for s in range(1, peers):
            total = total + slots[s]
        return total

    axes_z, axes_y, axes_x = (groups, on_z, g), (peers_y, on_y, at_y), (peers_x, on_x, me_x)

    def reduced(w, blocks):
        routes = ((axes_y, axes_z, axes_x), (axes_z, axes_y, axes_x))
        sums = [
            jnp.concatenate([pack(blocks[0]), pack(blocks[1])], axis=0),
            pack(blocks[2]),
        ]
        sent = []
        for hop in range(3):
            pending = []
            for way, total in enumerate(sums):
                peers, place, at = routes[way][hop]
                slots = (slots_a, slots_b)[way].at[w, hop]
                slots[at] = total
                copies = send_all(2 * w + way, hop, peers, place, slots.at[at], slots, at)
                pending.append((slots, peers, copies))
            yield None
            sums = []
            for slots, peers, copies in pending:
                for copy in copies:
                    copy.wait_recv()
                sent += copies
                sums.append(add_up(slots, peers))
        whole = [sums[0][:8], sums[0][8:], sums[1]]
        yield [unpack(line) * (1.0 / rows_total) for line in whole], sent

    lanes = work.shape[1]
    wide = lax.broadcasted_iota(jnp.int32, (rhs, lanes), 1)
    tall = lax.broadcasted_iota(jnp.int32, (rhs, lanes), 0)

    def factor(j, blocks):
        before = rhs * j
        corner = blocks[j]
        if j:
            left = exact_nt(jnp.concatenate(blocks[:j], axis=1), inv[:before, :before])
            corner = corner - exact_nt(left, left)
        work[...] = jnp.where(wide == tall + rhs, 1.0, 0.0)
        work[:, :rhs] = corner
        m = work[...]
        for p in range(rhs // 8):
            size = rhs - 8 * p
            cols = [jnp.broadcast_to(m[:, 8 * p + i : 8 * p + i + 1], (size, lanes)) for i in range(8)]
            for i in range(8):
                scale = lax.rsqrt(jnp.broadcast_to(cols[i][i : i + 1, :], (size, lanes)))
                column = cols[i] * scale
                line = jnp.broadcast_to(m[i : i + 1, :], (size, lanes)) * scale
                upper[8 * p + i : 8 * p + i + 1, :] = line[0:1, :]
                m = m - column * line
                for n in range(i + 1, 8):
                    cols[n] = cols[n] - column * jnp.broadcast_to(column[n : n + 1, :], (size, lanes))
            m = m[8:]
        square = lax.broadcasted_iota(jnp.int32, (rhs, rhs), 0)
        across = lax.broadcasted_iota(jnp.int32, (rhs, rhs), 1)
        r_ref[before : before + rhs, before : before + rhs] = jnp.where(
            across >= square, upper[:, :rhs], 0.0
        )
        corner_inv = upper[:, rhs : 2 * rhs]
        inv[before : before + rhs, before : before + rhs] = corner_inv
        if j:
            r_ref[:before, before : before + rhs] = left.T
            r_ref[before : before + rhs, :before] = jnp.zeros((rhs, before), F32)
            inv[before : before + rhs, :before] = -exact(corner_inv, exact(left, inv[:before, :before]))

    def project(j):
        width = rhs * (j + 1)
        rows = inv[rhs * j : width, :width]
        high = rows.astype(BF16)
        low = (rows - high.astype(F32)).astype(BF16)
        both = jnp.concatenate([high, low], axis=1)

        @pl.loop(0, column_cap, unroll=UN_PROJ)
        def _(c):
            stack = [vectors[i][c] for i in range(j + 1)]
            q_ref[0, c, rhs * j : width, :] = dot(both, jnp.concatenate(stack + stack, axis=0)).astype(BF16)

    halo_start(0)
    load_templates.wait()

    @pl.loop(0, tmpl.shape[0], unroll=4)
    def _(t):
        tmpl[t] = tmpl[t].T

    own_pass(0)
    layers_wait(0)
    layer_pass(0)
    plane_wait(0)
    ghost_pass(0)

    halo_start(1)
    early = reduced(0, gram((0, 1)))
    next(early)
    own_pass(1)
    layers_wait(1)
    layer_pass(1)
    next(early)
    plane_wait(1)
    ghost_pass(1)

    late = reduced(1, gram((2,)))
    next(late)
    next(early)
    next(late)
    (first, *second), sent_early = next(early)
    factor(0, [first])
    project(0)
    factor(1, second)
    next(late)
    project(1)
    third, sent_late = next(late)
    factor(2, third)
    project(2)
    halo_sent(0)
    halo_sent(1)
    for copy in sent_early + sent_late:
        copy.wait_send()


def solution(mesh):
    groups, pieces = mesh.shape["group"], mesh.shape["dom"]
    side = math.isqrt(pieces)
    peers_y = min(8, pieces // 2)
    peers_x = pieces // peers_y

    def body(basis_start, templates, template_ids, live_columns, face_refs, send_lists):
        _, column_cap, rhs, dof = basis_start.shape
        halo_cap = send_lists.shape[2]
        width = 3 * rhs
        lanes = 128
        rows_total = column_cap * dof * groups * pieces
        vmem, smem = pltpu.VMEM, pltpu.SMEM
        block = (rhs, dof)
        return pl.pallas_call(
            functools.partial(kernel, groups, side, peers_y, rows_total),
            out_shape=(
                jax.ShapeDtypeStruct((1, column_cap, width, dof), BF16),
                jax.ShapeDtypeStruct((width, width), F32),
            ),
            in_specs=[pl.BlockSpec(memory_space=pltpu.HBM)] * 2 + [pl.BlockSpec(memory_space=smem)] * 4,
            out_specs=(pl.BlockSpec(memory_space=vmem), pl.BlockSpec(memory_space=vmem)),
            scratch_shapes=[
                vmem(templates.shape, BF16),
                vmem((column_cap + 1, *block), BF16),
                vmem((column_cap + 1, *block), BF16),
                vmem((column_cap + 1, *block), BF16),
                vmem((8 * halo_cap + 1, *block), BF16),
                vmem((8 * halo_cap + 1, *block), BF16),
                vmem((8, halo_cap, *block), BF16),
                vmem((8, halo_cap, *block), BF16),
                vmem((2, column_cap, *block), BF16),
                vmem((2, column_cap, *block), BF16),
                vmem((column_cap, *block), F32),
                vmem((2, 3, 8, 16, lanes), F32),
                vmem((2, 3, 8, 8, lanes), F32),
                vmem((rhs, lanes), F32),
                vmem((rhs, lanes), F32),
                vmem((width, lanes), F32),
                pltpu.SemaphoreType.DMA((2,)),
                pltpu.SemaphoreType.DMA((2, 10)),
                pltpu.SemaphoreType.DMA((2, 10)),
                pltpu.SemaphoreType.DMA((4, 3, 8)),
                pltpu.SemaphoreType.DMA((4, 3, 8)),
            ],
            compiler_params=pltpu.CompilerParams(
                collective_id=0, has_side_effects=True, vmem_limit_bytes=40 * 2**20
            ),
        )(
            basis_start,
            templates,
            template_ids.transpose(2, 0, 1),
            live_columns,
            face_refs.T,
            send_lists.transpose(2, 0, 1),
        )

    return jax.shard_map(
        body,
        mesh=mesh,
        in_specs=(
            P("group", "dom", None, None),
            P(),
            P("group", "dom", None),
            P("dom"),
            P("dom", None),
            P("dom", None, None),
        ),
        out_specs=(P("group", "dom", None, None), P()),
        check_vma=False,
    )
```

```python
import functools
import math

import jax
import jax.numpy as jnp
from jax import lax
from jax.experimental import pallas as pl
from jax.experimental.pallas import tpu as pltpu
from jax.sharding import PartitionSpec as P

DIRECTIONS = ((-1, -1), (-1, 0), (-1, 1), (0, -1), (0, 1), (1, -1), (1, 0), (1, 1))
MESH = pl.DeviceIdType.MESH
F32 = jnp.float32
BF16 = jnp.bfloat16
NT = (((1,), (1,)), ((), ()))
HIGH = lax.Precision.HIGHEST
VMEM_MIB = 60
UN_OWN = UN_LAYER = UN_GHOST = UN_PROJ = 36
UN_GRAM = 18


def dot(x, y):
    return jnp.dot(x, y, preferred_element_type=F32)


def dot_nt(x, y):
    return lax.dot_general(x, y, NT, preferred_element_type=F32)


def exact(x, y):
    return jnp.dot(x, y, preferred_element_type=F32, precision=HIGH)


def exact_nt(x, y):
    return lax.dot_general(x, y, NT, preferred_element_type=F32, precision=HIGH)


def kernel(
    groups, side, peers_y, rows_total,
    basis_ref, templates_ref, ids_in, live_in, refs_in, lists_in,
    q_ref, r_ref,
    ids_ref, live_ref, refs_ref, lists_ref, tmpl, v0, v1, v2, ghost1, ghost2, packet1, packet2, layer1, layer2, acc,
    slots_a, slots_b, work, upper, inv,
    load_sem, halo_send, halo_recv, sum_send, sum_recv,
):
    column_cap, rhs, dof = v0.shape[0] - 1, v0.shape[1], v0.shape[2]
    halo_cap = packet1.shape[1]
    zero_own, zero_ghost = column_cap, 8 * halo_cap
    vectors, ghosts, layers = (v0, v1, v2), (ghost1, ghost2), (layer1, layer2)
    packets = (packet1, packet2)
    pieces = side * side
    peers_x = pieces // peers_y
    g = lax.axis_index("group")
    d = lax.axis_index("dom")
    row, col = d // side, d % side
    core, at_y, at_x = d % 2, (d // 2) % peers_y, d // (2 * peers_y)
    me_x = at_x * 2 + core

    def on_z(offset):
        return ((g + offset) % groups, d)

    def on_y(offset):
        return (g, (at_x * peers_y + (at_y + offset) % peers_y) * 2 + core)

    def on_x(offset):
        other = (me_x + offset) % peers_x
        return (g, ((other // 2) * peers_y + at_y) * 2 + other % 2)

    def inside(dx, dy):
        return (row + dx >= 0) & (row + dx < side) & (col + dy >= 0) & (col + dy < side)

    loads = [
        pltpu.make_async_copy(source, target, load_sem.at[2 + i])
        for i, (source, target) in enumerate(
            ((lists_in, lists_ref), (live_in, live_ref), (ids_in, ids_ref), (refs_in, refs_ref))
        )
    ]
    for load in loads:
        load.start()
    load_templates = pltpu.make_async_copy(templates_ref, tmpl, load_sem.at[0])
    load_templates.start()
    load_basis = pltpu.make_async_copy(basis_ref.at[0], v0.at[pl.ds(0, column_cap)], load_sem.at[1])
    load_basis.start()

    barrier = pltpu.get_barrier_semaphore()

    def greet(device):
        pl.semaphore_signal(barrier, inc=1, device_id=device, device_id_type=MESH)

    expected = 0
    for dx, dy in DIRECTIONS:
        target = (g, (row + dx) * side + col + dy)
        pl.when(inside(dx, dy))(functools.partial(greet, target))
        expected += inside(dx, dy).astype(jnp.int32)
    for peers, place in ((groups, on_z), (peers_y, on_y), (peers_x, on_x)):
        for offset in range(1, peers):
            greet(place(offset))
        expected += peers - 1

    empty = jnp.zeros((rhs, dof), BF16)
    for vector in vectors:
        vector[zero_own] = empty
    for x in range(2):
        ghosts[x][zero_ghost] = empty
        for k, (dx, dy) in enumerate(DIRECTIONS):
            @pl.when(jnp.logical_not(inside(-dx, -dy)))
            def _():
                ghosts[x][pl.ds(k * halo_cap, halo_cap)] = jnp.zeros((halo_cap, rhs, dof), BF16)

        @pl.when(g == 0)
        def _():
            layers[x][0] = jnp.zeros((column_cap, rhs, dof), BF16)

        @pl.when(g == groups - 1)
        def _():
            layers[x][1] = jnp.zeros((column_cap, rhs, dof), BF16)

    inv[...] = jnp.zeros(inv.shape, F32)
    for load in loads:
        load.wait()
    live = live_ref[0]
    load_basis.wait()

    @pl.loop(0, column_cap)
    def _(c):
        v0[c] = v0[c] * (c < live).astype(F32).astype(BF16)

    pl.semaphore_wait(barrier, expected)

    def plane_copy(x, k):
        dx, dy = DIRECTIONS[k]
        return pltpu.make_async_remote_copy(
            src_ref=packets[x].at[k],
            dst_ref=ghosts[x].at[pl.ds(k * halo_cap, halo_cap)],
            send_sem=halo_send.at[x, k],
            recv_sem=halo_recv.at[x, k],
            device_id=(g, (row + dx) * side + col + dy),
            device_id_type=MESH,
        )

    def layer_copy(x, up):
        return pltpu.make_async_remote_copy(
            src_ref=vectors[x].at[pl.ds(0, column_cap)],
            dst_ref=layers[x].at[0 if up else 1],
            send_sem=halo_send.at[x, 8 + up],
            recv_sem=halo_recv.at[x, 8 + up],
            device_id=(g + 1 if up else g - 1, d),
            device_id_type=MESH,
        )

    has_up, has_down = g < groups - 1, g > 0
    order = (6, 1, 5, 7, 0, 2, 3, 4)

    def halo_start(x):
        vector = vectors[x]
        for k in order:
            if k == 3:
                pl.when(has_up)(lambda: layer_copy(x, 1).start())
                pl.when(has_down)(lambda: layer_copy(x, 0).start())
            for s in range(halo_cap):
                slot = lists_ref[s, 0, k]
                packets[x][k, s] = vector[jnp.where(slot < 0, zero_own, slot)]
            pl.when(inside(*DIRECTIONS[k]))(lambda: plane_copy(x, k).start())

    def layers_wait(x):
        pl.when(has_down)(lambda: layer_copy(x, 1).wait_recv())
        pl.when(has_up)(lambda: layer_copy(x, 0).wait_recv())

    def plane_wait(x):
        for k in order:
            dx, dy = DIRECTIONS[k]
            pl.when(inside(-dx, -dy))(lambda: plane_copy(x, k).wait_recv())

    def halo_sent(x):
        for k in order:
            pl.when(inside(*DIRECTIONS[k]))(lambda: plane_copy(x, k).wait_send())
        pl.when(has_up)(lambda: layer_copy(x, 1).wait_send())
        pl.when(has_down)(lambda: layer_copy(x, 0).wait_send())

    def apply(blocks, c, faces):
        weights = jnp.concatenate([tmpl[ids_ref[f, 0, c]] for f in faces], axis=0)
        return dot(jnp.concatenate(blocks, axis=1), weights)

    def own_pass(x):
        vector = vectors[x]

        @pl.loop(0, column_cap, unroll=UN_OWN)
        def _(c):
            blocks = [vector[c]]
            for q in range(4):
                r = refs_ref[q, c]
                blocks.append(vector[jnp.where((r < 0) | (r >= column_cap), zero_own, r)])
            acc[c] = apply(blocks, c, (0, 3, 4, 5, 6))

    def layer_pass(x):
        @pl.loop(0, column_cap, unroll=UN_LAYER)
        def _(c):
            acc[c] = acc[c] + apply([layers[x][0, c], layers[x][1, c]], c, (1, 2))

    def ghost_pass(x):
        @pl.loop(0, column_cap, unroll=UN_GHOST)
        def _(c):
            blocks = []
            for q in range(4):
                r = refs_ref[q, c]
                blocks.append(ghosts[x][jnp.where(r < column_cap, zero_ghost, r - column_cap)])
            total = acc[c] + apply(blocks, c, (3, 4, 5, 6))
            vectors[x + 1][c] = jnp.where(c < live, total, 0.0).astype(BF16)

    def gram(rows):
        def add(h, carry):
            pair = [
                jnp.concatenate([vectors[i][2 * h], vectors[i][2 * h + 1]], axis=1)
                for i in range(rows[-1] + 1)
            ]
            return tuple(
                total + dot_nt(pair[j], jnp.concatenate(pair[: j + 1], axis=0))
                for j, total in zip(rows, carry)
            )

        start = tuple(jnp.zeros((rhs, rhs * (j + 1)), F32) for j in rows)
        totals = lax.fori_loop(0, column_cap // 2, add, start, unroll=UN_GRAM)
        return [t[:, rhs * i : rhs * (i + 1)] for t in totals for i in range(t.shape[1] // rhs)]

    def pack(block):
        return jnp.concatenate([block[8 * i : 8 * i + 8] for i in range(rhs // 8)], axis=1)

    def unpack(line):
        return jnp.concatenate([line[:, rhs * i : rhs * (i + 1)] for i in range(rhs // 8)], axis=0)

    def send_all(w, hop, peers, place, source, slots, at):
        copies = [
            pltpu.make_async_remote_copy(
                src_ref=source,
                dst_ref=slots.at[at],
                send_sem=sum_send.at[w, hop, offset],
                recv_sem=sum_recv.at[w, hop, offset],
                device_id=place(offset),
                device_id_type=MESH,
            )
            for offset in range(1, peers)
        ]
        for copy in copies:
            copy.start()
        return copies

    def add_up(slots, peers):
        total = slots[0]
        for s in range(1, peers):
            total = total + slots[s]
        return total

    axes_z, axes_y, axes_x = (groups, on_z, g), (peers_y, on_y, at_y), (peers_x, on_x, me_x)

    def reduced(w, blocks):
        routes = ((axes_y, axes_z, axes_x), (axes_z, axes_y, axes_x))
        sums = [
            jnp.concatenate([pack(blocks[0]), pack(blocks[1])], axis=0),
            pack(blocks[2]),
        ]
        sent = []
        for hop in range(3):
            pending = []
            for way, total in enumerate(sums):
                peers, place, at = routes[way][hop]
                slots = (slots_a, slots_b)[way].at[w, hop]
                slots[at] = total
                copies = send_all(2 * w + way, hop, peers, place, slots.at[at], slots, at)
                pending.append((slots, peers, copies))
            yield None
            sums = []
            for slots, peers, copies in pending:
                for copy in copies:
                    copy.wait_recv()
                sent += copies
                sums.append(add_up(slots, peers))
        whole = [sums[0][:8], sums[0][8:], sums[1]]
        yield [unpack(line) * (1.0 / rows_total) for line in whole], sent

    lanes = work.shape[1]
    wide = lax.broadcasted_iota(jnp.int32, (rhs, lanes), 1)
    tall = lax.broadcasted_iota(jnp.int32, (rhs, lanes), 0)

    def factor(j, blocks):
        before = rhs * j
        corner = blocks[j]
        if j:
            left = exact_nt(jnp.concatenate(blocks[:j], axis=1), inv[:before, :before])
            corner = corner - exact_nt(left, left)
        work[...] = jnp.where(wide == tall + rhs, 1.0, 0.0)
        work[:, :rhs] = corner
        m = work[...]
        for p in range(rhs // 8):
            size = rhs - 8 * p
            cols = [jnp.broadcast_to(m[:, 8 * p + i : 8 * p + i + 1], (size, lanes)) for i in range(8)]
            for i in range(8):
                scale = lax.rsqrt(jnp.broadcast_to(cols[i][i : i + 1, :], (size, lanes)))
                column = cols[i] * scale
                line = jnp.broadcast_to(m[i : i + 1, :], (size, lanes)) * scale
                upper[8 * p + i : 8 * p + i + 1, :] = line[0:1, :]
                m = m - column * line
                for n in range(i + 1, 8):
                    cols[n] = cols[n] - column * jnp.broadcast_to(column[n : n + 1, :], (size, lanes))
            m = m[8:]
        square = lax.broadcasted_iota(jnp.int32, (rhs, rhs), 0)
        across = lax.broadcasted_iota(jnp.int32, (rhs, rhs), 1)
        r_ref[before : before + rhs, before : before + rhs] = jnp.where(
            across >= square, upper[:, :rhs], 0.0
        )
        corner_inv = upper[:, rhs : 2 * rhs]
        inv[before : before + rhs, before : before + rhs] = corner_inv
        if j:
            r_ref[:before, before : before + rhs] = left.T
            r_ref[before : before + rhs, :before] = jnp.zeros((rhs, before), F32)
            inv[before : before + rhs, :before] = -exact(corner_inv, exact(left, inv[:before, :before]))

    def project(j):
        width = rhs * (j + 1)
        rows = inv[rhs * j : width, :width]
        high = rows.astype(BF16)
        low = (rows - high.astype(F32)).astype(BF16)
        both = jnp.concatenate([high, low], axis=1)

        @pl.loop(0, column_cap, unroll=UN_PROJ)
        def _(c):
            stack = [vectors[i][c] for i in range(j + 1)]
            q_ref[0, c, rhs * j : width, :] = dot(both, jnp.concatenate(stack + stack, axis=0)).astype(BF16)

    halo_start(0)
    load_templates.wait()

    @pl.loop(0, tmpl.shape[0], unroll=4)
    def _(t):
        tmpl[t] = tmpl[t].T

    own_pass(0)
    layers_wait(0)
    layer_pass(0)
    plane_wait(0)
    ghost_pass(0)

    halo_start(1)
    early = reduced(0, gram((0, 1)))
    next(early)
    own_pass(1)
    layers_wait(1)
    layer_pass(1)
    next(early)
    plane_wait(1)
    ghost_pass(1)

    late = reduced(1, gram((2,)))
    next(late)
    next(early)
    next(late)
    (first, *second), sent_early = next(early)
    factor(0, [first])
    project(0)
    factor(1, second)
    next(late)
    project(1)
    third, sent_late = next(late)
    factor(2, third)
    project(2)
    halo_sent(0)
    halo_sent(1)
    for copy in sent_early + sent_late:
        copy.wait_send()


def solution(mesh):
    groups, pieces = mesh.shape["group"], mesh.shape["dom"]
    side = math.isqrt(pieces)
    peers_y = min(8, pieces // 2)
    peers_x = pieces // peers_y

    def body(basis_start, templates, template_ids, live_columns, face_refs, send_lists):
        _, column_cap, rhs, dof = basis_start.shape
        halo_cap = send_lists.shape[2]
        faces = template_ids.shape[2]
        width = 3 * rhs
        lanes = 128
        rows_total = column_cap * dof * groups * pieces
        vmem, smem = pltpu.VMEM, pltpu.SMEM
        block = (rhs, dof)
        return pl.pallas_call(
            functools.partial(kernel, groups, side, peers_y, rows_total),
            out_shape=(
                jax.ShapeDtypeStruct((1, column_cap, width, dof), BF16),
                jax.ShapeDtypeStruct((width, width), F32),
            ),
            in_specs=[pl.BlockSpec(memory_space=pltpu.HBM)] * 6,
            out_specs=(pl.BlockSpec(memory_space=vmem), pl.BlockSpec(memory_space=vmem)),
            scratch_shapes=[
                smem((faces, 1, column_cap), jnp.int32),
                smem((1,), jnp.int32),
                smem((4, column_cap), jnp.int32),
                smem((halo_cap, 1, 8), jnp.int32),
                vmem(templates.shape, BF16),
                vmem((column_cap + 1, *block), BF16),
                vmem((column_cap + 1, *block), BF16),
                vmem((column_cap + 1, *block), BF16),
                vmem((8 * halo_cap + 1, *block), BF16),
                vmem((8 * halo_cap + 1, *block), BF16),
                vmem((8, halo_cap, *block), BF16),
                vmem((8, halo_cap, *block), BF16),
                vmem((2, column_cap, *block), BF16),
                vmem((2, column_cap, *block), BF16),
                vmem((column_cap, *block), F32),
                vmem((2, 3, 8, 16, lanes), F32),
                vmem((2, 3, 8, 8, lanes), F32),
                vmem((rhs, lanes), F32),
                vmem((rhs, lanes), F32),
                vmem((width, lanes), F32),
                pltpu.SemaphoreType.DMA((6,)),
                pltpu.SemaphoreType.DMA((2, 10)),
                pltpu.SemaphoreType.DMA((2, 10)),
                pltpu.SemaphoreType.DMA((4, 3, 8)),
                pltpu.SemaphoreType.DMA((4, 3, 8)),
            ],
            compiler_params=pltpu.CompilerParams(
                collective_id=0, has_side_effects=True, vmem_limit_bytes=VMEM_MIB * 2**20
            ),
        )(
            basis_start,
            templates,
            template_ids.transpose(2, 0, 1),
            live_columns,
            face_refs.T,
            send_lists.transpose(2, 0, 1),
        )

    return jax.shard_map(
        body,
        mesh=mesh,
        in_specs=(
            P("group", "dom", None, None),
            P(),
            P("group", "dom", None),
            P("dom"),
            P("dom", None),
            P("dom", None, None),
        ),
        out_specs=(P("group", "dom", None, None), P()),
        check_vma=False,
    )
```

```python
import functools
import math

import jax
import jax.numpy as jnp
from jax import lax
from jax.experimental import pallas as pl
from jax.experimental.pallas import tpu as pltpu
from jax.sharding import PartitionSpec as P

DIRECTIONS = ((-1, -1), (-1, 0), (-1, 1), (0, -1), (0, 1), (1, -1), (1, 0), (1, 1))
ORDER = (6, 1, 5, 7, 0, 2, 3, 4)
MESH = pl.DeviceIdType.MESH
F32 = jnp.float32
BF16 = jnp.bfloat16
NT = (((1,), (1,)), ((), ()))
HIGH = lax.Precision.HIGHEST
VMEM_MIB = 58
UN_OWN = UN_LAYER = UN_GHOST = UN_PROJ = 36
UN_GRAM = 18


def dot(x, y):
    return jnp.dot(x, y, preferred_element_type=F32)


def dot_nt(x, y):
    return lax.dot_general(x, y, NT, preferred_element_type=F32)


def exact(x, y):
    return jnp.dot(x, y, preferred_element_type=F32, precision=HIGH)


def exact_nt(x, y):
    return lax.dot_general(x, y, NT, preferred_element_type=F32, precision=HIGH)


def kernel(
    groups, side, peers_y, rows_total,
    basis_ref, templates_ref, ids_in, live_in, refs_in, lists_in,
    q_ref, r_ref,
    ids_ref, live_ref, refs_ref, lists_ref, tmpl, v0, v1, v2, ghost1, ghost2, packet1, packet2, layer1, layer2, acc,
    slots_a, slots_b, work, upper, inv,
    load_sem, halo_send, halo_recv, sum_send, sum_recv,
):
    column_cap, rhs, dof = v0.shape[0] - 1, v0.shape[1], v0.shape[2]
    halo_cap = packet1.shape[1]
    zero_own, zero_ghost = column_cap, 8 * halo_cap
    vectors, ghosts, layers = (v0, v1, v2), (ghost1, ghost2), (layer1, layer2)
    packets = (packet1, packet2)
    pieces = side * side
    peers_x = pieces // peers_y
    g = lax.axis_index("group")
    d = lax.axis_index("dom")
    row, col = d // side, d % side
    core, at_y, at_x = d % 2, (d // 2) % peers_y, d // (2 * peers_y)
    me_x = at_x * 2 + core

    def on_z(offset):
        return ((g + offset) % groups, d)

    def on_y(offset):
        return (g, (at_x * peers_y + (at_y + offset) % peers_y) * 2 + core)

    def on_x(offset):
        other = (me_x + offset) % peers_x
        return (g, ((other // 2) * peers_y + at_y) * 2 + other % 2)

    def inside(dx, dy):
        return (row + dx >= 0) & (row + dx < side) & (col + dy >= 0) & (col + dy < side)

    barrier = pltpu.get_barrier_semaphore()

    def greet(device):
        pl.semaphore_signal(barrier, inc=1, device_id=device, device_id_type=MESH)

    expected = 0
    for dx, dy in (DIRECTIONS[k] for k in ORDER):
        target = (g, (row + dx) * side + col + dy)
        pl.when(inside(dx, dy))(functools.partial(greet, target))
        expected += inside(dx, dy).astype(jnp.int32)
    for peers, place in ((groups, on_z), (peers_y, on_y), (peers_x, on_x)):
        for offset in range(1, peers):
            greet(place(offset))
        expected += peers - 1

    loads = [
        pltpu.make_async_copy(source, target, load_sem.at[2 + i])
        for i, (source, target) in enumerate(
            ((lists_in, lists_ref), (live_in, live_ref), (ids_in, ids_ref), (refs_in, refs_ref))
        )
    ]
    for load in loads:
        load.start()
    load_templates = pltpu.make_async_copy(templates_ref, tmpl, load_sem.at[0])
    load_templates.start()
    load_basis = pltpu.make_async_copy(basis_ref.at[0], v0.at[pl.ds(0, column_cap)], load_sem.at[1])
    load_basis.start()

    empty = jnp.zeros((rhs, dof), BF16)
    for vector in vectors:
        vector[zero_own] = empty
    for x in range(2):
        ghosts[x][zero_ghost] = empty
        for k, (dx, dy) in enumerate(DIRECTIONS):
            @pl.when(jnp.logical_not(inside(-dx, -dy)))
            def _():
                ghosts[x][pl.ds(k * halo_cap, halo_cap)] = jnp.zeros((halo_cap, rhs, dof), BF16)

        @pl.when(g == 0)
        def _():
            layers[x][0] = jnp.zeros((column_cap, rhs, dof), BF16)

        @pl.when(g == groups - 1)
        def _():
            layers[x][1] = jnp.zeros((column_cap, rhs, dof), BF16)

    inv[...] = jnp.zeros(inv.shape, F32)
    for load in loads:
        load.wait()
    live = live_ref[0]
    load_basis.wait()

    @pl.loop(0, column_cap)
    def _(c):
        v0[c] = v0[c] * (c < live).astype(F32).astype(BF16)

    def plane_copy(x, k):
        dx, dy = DIRECTIONS[k]
        return pltpu.make_async_remote_copy(
            src_ref=packets[x].at[k],
            dst_ref=ghosts[x].at[pl.ds(k * halo_cap, halo_cap)],
            send_sem=halo_send.at[x, k],
            recv_sem=halo_recv.at[x, k],
            device_id=(g, (row + dx) * side + col + dy),
            device_id_type=MESH,
        )

    def layer_copy(x, up):
        return pltpu.make_async_remote_copy(
            src_ref=vectors[x].at[pl.ds(0, column_cap)],
            dst_ref=layers[x].at[0 if up else 1],
            send_sem=halo_send.at[x, 8 + up],
            recv_sem=halo_recv.at[x, 8 + up],
            device_id=(g + 1 if up else g - 1, d),
            device_id_type=MESH,
        )

    has_up, has_down = g < groups - 1, g > 0

    def pack_packet(x, k):
        for s in range(halo_cap):
            slot = lists_ref[s, 0, k]
            packets[x][k, s] = vectors[x][jnp.where(slot < 0, zero_own, slot)]

    def halo_start(x, packed):
        for k in ORDER:
            if k == 3:
                pl.when(has_up)(lambda: layer_copy(x, 1).start())
                pl.when(has_down)(lambda: layer_copy(x, 0).start())
            if not packed:
                pack_packet(x, k)
            pl.when(inside(*DIRECTIONS[k]))(lambda: plane_copy(x, k).start())

    def layers_wait(x):
        pl.when(has_down)(lambda: layer_copy(x, 1).wait_recv())
        pl.when(has_up)(lambda: layer_copy(x, 0).wait_recv())

    def plane_wait(x):
        for k in ORDER:
            dx, dy = DIRECTIONS[k]
            pl.when(inside(-dx, -dy))(lambda: plane_copy(x, k).wait_recv())

    def halo_sent(x):
        for k in ORDER:
            pl.when(inside(*DIRECTIONS[k]))(lambda: plane_copy(x, k).wait_send())
        pl.when(has_up)(lambda: layer_copy(x, 1).wait_send())
        pl.when(has_down)(lambda: layer_copy(x, 0).wait_send())

    def apply(blocks, c, faces):
        weights = jnp.concatenate([tmpl[ids_ref[f, 0, c]] for f in faces], axis=0)
        return dot(jnp.concatenate(blocks, axis=1), weights)

    def own_pass(x):
        vector = vectors[x]

        @pl.loop(0, column_cap, unroll=UN_OWN)
        def _(c):
            blocks = [vector[c]]
            for q in range(4):
                r = refs_ref[q, c]
                blocks.append(vector[jnp.where((r < 0) | (r >= column_cap), zero_own, r)])
            acc[c] = apply(blocks, c, (0, 3, 4, 5, 6))

    def layer_pass(x):
        @pl.loop(0, column_cap, unroll=UN_LAYER)
        def _(c):
            acc[c] = acc[c] + apply([layers[x][0, c], layers[x][1, c]], c, (1, 2))

    def ghost_pass(x):
        @pl.loop(0, column_cap, unroll=UN_GHOST)
        def _(c):
            blocks = []
            for q in range(4):
                r = refs_ref[q, c]
                blocks.append(ghosts[x][jnp.where(r < column_cap, zero_ghost, r - column_cap)])
            total = acc[c] + apply(blocks, c, (3, 4, 5, 6))
            vectors[x + 1][c] = jnp.where(c < live, total, 0.0).astype(BF16)

    def gram(rows):
        def add(h, carry):
            pair = [
                jnp.concatenate([vectors[i][2 * h], vectors[i][2 * h + 1]], axis=1)
                for i in range(rows[-1] + 1)
            ]
            return tuple(
                total + dot_nt(pair[j], jnp.concatenate(pair[: j + 1], axis=0))
                for j, total in zip(rows, carry)
            )

        start = tuple(jnp.zeros((rhs, rhs * (j + 1)), F32) for j in rows)
        totals = lax.fori_loop(0, column_cap // 2, add, start, unroll=UN_GRAM)
        return [t[:, rhs * i : rhs * (i + 1)] for t in totals for i in range(t.shape[1] // rhs)]

    def pack(block):
        return jnp.concatenate([block[8 * i : 8 * i + 8] for i in range(rhs // 8)], axis=1)

    def unpack(line):
        return jnp.concatenate([line[:, rhs * i : rhs * (i + 1)] for i in range(rhs // 8)], axis=0)

    def send_all(w, hop, peers, place, source, slots, at):
        copies = [
            pltpu.make_async_remote_copy(
                src_ref=source,
                dst_ref=slots.at[at],
                send_sem=sum_send.at[w, hop, offset],
                recv_sem=sum_recv.at[w, hop, offset],
                device_id=place(offset),
                device_id_type=MESH,
            )
            for offset in range(1, peers)
        ]
        for copy in copies:
            copy.start()
        return copies

    def add_up(slots, peers):
        total = slots[0]
        for s in range(1, peers):
            total = total + slots[s]
        return total

    axes_z, axes_y, axes_x = (groups, on_z, g), (peers_y, on_y, at_y), (peers_x, on_x, me_x)

    def reduced(w, blocks):
        routes = ((axes_y, axes_z, axes_x), (axes_z, axes_y, axes_x))
        sums = [
            jnp.concatenate([pack(blocks[0]), pack(blocks[1])], axis=0),
            pack(blocks[2]),
        ]
        sent = []
        for hop in range(3):
            pending = []
            for way, total in enumerate(sums):
                peers, place, at = routes[way][hop]
                slots = (slots_a, slots_b)[way].at[w, hop]
                slots[at] = total
                copies = send_all(2 * w + way, hop, peers, place, slots.at[at], slots, at)
                pending.append((slots, peers, copies))
            yield None
            sums = []
            for slots, peers, copies in pending:
                for copy in copies:
                    copy.wait_recv()
                sent += copies
                sums.append(add_up(slots, peers))
        whole = [sums[0][:8], sums[0][8:], sums[1]]
        yield [unpack(line) * (1.0 / rows_total) for line in whole], sent

    lanes = work.shape[1]
    wide = lax.broadcasted_iota(jnp.int32, (rhs, lanes), 1)
    tall = lax.broadcasted_iota(jnp.int32, (rhs, lanes), 0)

    def factor(j, blocks):
        before = rhs * j
        corner = blocks[j]
        if j:
            left = exact_nt(jnp.concatenate(blocks[:j], axis=1), inv[:before, :before])
            corner = corner - exact_nt(left, left)
            across_inv = exact(left, inv[:before, :before])
        work[...] = jnp.where(wide == tall + rhs, 1.0, 0.0)
        work[:, :rhs] = corner
        m = work[...]
        for p in range(rhs // 8):
            size = rhs - 8 * p
            cols = [jnp.broadcast_to(m[:, 8 * p + i : 8 * p + i + 1], (size, lanes)) for i in range(8)]
            for i in range(8):
                scale = lax.rsqrt(jnp.broadcast_to(cols[i][i : i + 1, :], (size, lanes)))
                column = cols[i] * scale
                line = jnp.broadcast_to(m[i : i + 1, :], (size, lanes)) * scale
                upper[8 * p + i : 8 * p + i + 1, :] = line[0:1, :]
                m = m - column * line
                for n in range(i + 1, 8):
                    cols[n] = cols[n] - column * jnp.broadcast_to(column[n : n + 1, :], (size, lanes))
            m = m[8:]
        square = lax.broadcasted_iota(jnp.int32, (rhs, rhs), 0)
        across = lax.broadcasted_iota(jnp.int32, (rhs, rhs), 1)
        r_ref[before : before + rhs, before : before + rhs] = jnp.where(
            across >= square, upper[:, :rhs], 0.0
        )
        corner_inv = upper[:, rhs : 2 * rhs]
        inv[before : before + rhs, before : before + rhs] = corner_inv
        if j:
            r_ref[:before, before : before + rhs] = left.T
            r_ref[before : before + rhs, :before] = jnp.zeros((rhs, before), F32)
            inv[before : before + rhs, :before] = -exact(corner_inv, across_inv)

    def project(j):
        width = rhs * (j + 1)
        rows = inv[rhs * j : width, :width]
        high = rows.astype(BF16)
        low = (rows - high.astype(F32)).astype(BF16)
        both = jnp.concatenate([high, low], axis=1)

        @pl.loop(0, column_cap, unroll=UN_PROJ)
        def _(c):
            stack = [vectors[i][c] for i in range(j + 1)]
            q_ref[0, c, rhs * j : width, :] = dot(both, jnp.concatenate(stack + stack, axis=0)).astype(BF16)

    for k in ORDER:
        pack_packet(0, k)
    pl.semaphore_wait(barrier, expected)
    halo_start(0, True)
    load_templates.wait()

    @pl.loop(0, tmpl.shape[0], unroll=4)
    def _(t):
        tmpl[t] = tmpl[t].T

    own_pass(0)
    layers_wait(0)
    layer_pass(0)
    plane_wait(0)
    ghost_pass(0)

    halo_start(1, False)
    early = reduced(0, gram((0, 1)))
    next(early)
    own_pass(1)
    layers_wait(1)
    layer_pass(1)
    next(early)
    plane_wait(1)
    ghost_pass(1)

    late = reduced(1, gram((2,)))
    next(late)
    next(early)
    next(late)
    (first, *second), sent_early = next(early)
    factor(0, [first])
    project(0)
    factor(1, second)
    next(late)
    project(1)
    third, sent_late = next(late)
    factor(2, third)
    project(2)
    halo_sent(0)
    halo_sent(1)
    for copy in sent_early + sent_late:
        copy.wait_send()


def solution(mesh):
    groups, pieces = mesh.shape["group"], mesh.shape["dom"]
    side = math.isqrt(pieces)
    peers_y = min(8, pieces // 2)
    peers_x = pieces // peers_y

    def body(basis_start, templates, template_ids, live_columns, face_refs, send_lists):
        _, column_cap, rhs, dof = basis_start.shape
        halo_cap = send_lists.shape[2]
        faces = template_ids.shape[2]
        width = 3 * rhs
        lanes = 128
        rows_total = column_cap * dof * groups * pieces
        vmem, smem = pltpu.VMEM, pltpu.SMEM
        block = (rhs, dof)
        return pl.pallas_call(
            functools.partial(kernel, groups, side, peers_y, rows_total),
            out_shape=(
                vmem((1, column_cap, width, dof), BF16),
                vmem((width, width), F32),
            ),
            in_specs=[pl.BlockSpec(memory_space=pltpu.HBM)] * 6,
            out_specs=(pl.BlockSpec(memory_space=vmem), pl.BlockSpec(memory_space=vmem)),
            scratch_shapes=[
                smem((faces, 1, column_cap), jnp.int32),
                smem((1,), jnp.int32),
                smem((4, column_cap), jnp.int32),
                smem((halo_cap, 1, 8), jnp.int32),
                vmem(templates.shape, BF16),
                vmem((column_cap + 1, *block), BF16),
                vmem((column_cap + 1, *block), BF16),
                vmem((column_cap + 1, *block), BF16),
                vmem((8 * halo_cap + 1, *block), BF16),
                vmem((8 * halo_cap + 1, *block), BF16),
                vmem((8, halo_cap, *block), BF16),
                vmem((8, halo_cap, *block), BF16),
                vmem((2, column_cap, *block), BF16),
                vmem((2, column_cap, *block), BF16),
                vmem((column_cap, *block), F32),
                vmem((2, 3, 8, 16, lanes), F32),
                vmem((2, 3, 8, 8, lanes), F32),
                vmem((rhs, lanes), F32),
                vmem((rhs, lanes), F32),
                vmem((width, lanes), F32),
                pltpu.SemaphoreType.DMA((6,)),
                pltpu.SemaphoreType.DMA((2, 10)),
                pltpu.SemaphoreType.DMA((2, 10)),
                pltpu.SemaphoreType.DMA((4, 3, 8)),
                pltpu.SemaphoreType.DMA((4, 3, 8)),
            ],
            compiler_params=pltpu.CompilerParams(
                collective_id=0, has_side_effects=True, vmem_limit_bytes=VMEM_MIB * 2**20
            ),
        )(
            basis_start,
            templates,
            template_ids.transpose(2, 0, 1),
            live_columns,
            face_refs.T,
            send_lists.transpose(2, 0, 1),
        )

    return jax.shard_map(
        body,
        mesh=mesh,
        in_specs=(
            P("group", "dom", None, None),
            P(),
            P("group", "dom", None),
            P("dom"),
            P("dom", None),
            P("dom", None, None),
        ),
        out_specs=(P("group", "dom", None, None), P()),
        check_vma=False,
    )
```

```python
import functools
import math

import jax
import jax.numpy as jnp
from jax import lax
from jax.experimental import pallas as pl
from jax.experimental.pallas import tpu as pltpu
from jax.sharding import PartitionSpec as P

DIRECTIONS = ((-1, -1), (-1, 0), (-1, 1), (0, -1), (0, 1), (1, -1), (1, 0), (1, 1))
ORDER = (6, 1, 5, 7, 0, 2, 3, 4)
MESH = pl.DeviceIdType.MESH
F32 = jnp.float32
BF16 = jnp.bfloat16
NT = (((1,), (1,)), ((), ()))
HIGH = lax.Precision.HIGHEST
CORNER_CAP = 2
VMEM_MIB = 58
UN_OWN = UN_LAYER = UN_GHOST = UN_PROJ = 36
UN_GRAM = 18


def dot(x, y):
    return jnp.dot(x, y, preferred_element_type=F32)


def dot_nt(x, y):
    return lax.dot_general(x, y, NT, preferred_element_type=F32)


def exact(x, y):
    return jnp.dot(x, y, preferred_element_type=F32, precision=HIGH)


def exact_nt(x, y):
    return lax.dot_general(x, y, NT, preferred_element_type=F32, precision=HIGH)


def kernel(
    groups, side, peers_y, rows_total, caps,
    basis_ref, templates_ref, ids_in, live_in, refs_in, lists_in,
    q_ref, r_ref,
    ids_ref, live_ref, refs_ref, lists_ref, tmpl, v0, v1, v2, ghost1, ghost2, packet1, packet2, layer1, layer2, acc,
    slots_a, slots_b, work, upper, inv,
    load_sem, halo_send, halo_recv, sum_send, sum_recv,
):
    column_cap, rhs, dof = v0.shape[0] - 1, v0.shape[1], v0.shape[2]
    halo_cap = packet1.shape[1]
    zero_own, zero_ghost = column_cap, 8 * halo_cap
    vectors, ghosts, layers = (v0, v1, v2), (ghost1, ghost2), (layer1, layer2)
    packets = (packet1, packet2)
    pieces = side * side
    peers_x = pieces // peers_y
    g = lax.axis_index("group")
    d = lax.axis_index("dom")
    row, col = d // side, d % side
    core, at_y, at_x = d % 2, (d // 2) % peers_y, d // (2 * peers_y)
    me_x = at_x * 2 + core

    def on_z(offset):
        return ((g + offset) % groups, d)

    def on_y(offset):
        return (g, (at_x * peers_y + (at_y + offset) % peers_y) * 2 + core)

    def on_x(offset):
        other = (me_x + offset) % peers_x
        return (g, ((other // 2) * peers_y + at_y) * 2 + other % 2)

    def inside(dx, dy):
        return (row + dx >= 0) & (row + dx < side) & (col + dy >= 0) & (col + dy < side)

    barrier = pltpu.get_barrier_semaphore()

    def greet(device):
        pl.semaphore_signal(barrier, inc=1, device_id=device, device_id_type=MESH)

    expected = 0
    for dx, dy in (DIRECTIONS[k] for k in ORDER):
        target = (g, (row + dx) * side + col + dy)
        pl.when(inside(dx, dy))(functools.partial(greet, target))
        expected += inside(dx, dy).astype(jnp.int32)
    for peers, place in ((groups, on_z), (peers_y, on_y), (peers_x, on_x)):
        for offset in range(1, peers):
            greet(place(offset))
        expected += peers - 1

    loads = [
        pltpu.make_async_copy(source, target, load_sem.at[2 + i])
        for i, (source, target) in enumerate(
            ((lists_in, lists_ref), (live_in, live_ref), (ids_in, ids_ref), (refs_in, refs_ref))
        )
    ]
    for load in loads:
        load.start()
    load_templates = pltpu.make_async_copy(templates_ref, tmpl, load_sem.at[0])
    load_templates.start()
    load_basis = pltpu.make_async_copy(basis_ref.at[0], v0.at[pl.ds(0, column_cap)], load_sem.at[1])
    load_basis.start()

    empty = jnp.zeros((rhs, dof), BF16)
    for vector in vectors:
        vector[zero_own] = empty
    for x in range(2):
        ghosts[x][zero_ghost] = empty
        for k, (dx, dy) in enumerate(DIRECTIONS):
            @pl.when(jnp.logical_not(inside(-dx, -dy)))
            def _():
                ghosts[x][pl.ds(k * halo_cap, halo_cap)] = jnp.zeros((halo_cap, rhs, dof), BF16)

        @pl.when(g == 0)
        def _():
            layers[x][0] = jnp.zeros((column_cap, rhs, dof), BF16)

        @pl.when(g == groups - 1)
        def _():
            layers[x][1] = jnp.zeros((column_cap, rhs, dof), BF16)

    inv[...] = jnp.zeros(inv.shape, F32)
    for load in loads:
        load.wait()
    live = live_ref[0]
    load_basis.wait()

    @pl.loop(0, column_cap)
    def _(c):
        v0[c] = v0[c] * (c < live).astype(F32).astype(BF16)

    def plane_copy(x, k):
        dx, dy = DIRECTIONS[k]
        return pltpu.make_async_remote_copy(
            src_ref=packets[x].at[k, pl.ds(0, caps[k])],
            dst_ref=ghosts[x].at[pl.ds(k * halo_cap, caps[k])],
            send_sem=halo_send.at[x, k],
            recv_sem=halo_recv.at[x, k],
            device_id=(g, (row + dx) * side + col + dy),
            device_id_type=MESH,
        )

    def layer_copy(x, up):
        return pltpu.make_async_remote_copy(
            src_ref=vectors[x].at[pl.ds(0, column_cap)],
            dst_ref=layers[x].at[0 if up else 1],
            send_sem=halo_send.at[x, 8 + up],
            recv_sem=halo_recv.at[x, 8 + up],
            device_id=(g + 1 if up else g - 1, d),
            device_id_type=MESH,
        )

    has_up, has_down = g < groups - 1, g > 0

    def pack_packet(x, k):
        for s in range(caps[k]):
            slot = lists_ref[s, 0, k]
            packets[x][k, s] = vectors[x][jnp.where(slot < 0, zero_own, slot)]

    def halo_start(x, packed):
        for k in ORDER:
            if k == 3:
                pl.when(has_up)(lambda: layer_copy(x, 1).start())
                pl.when(has_down)(lambda: layer_copy(x, 0).start())
            if not packed:
                pack_packet(x, k)
            pl.when(inside(*DIRECTIONS[k]))(lambda: plane_copy(x, k).start())

    def layers_wait(x):
        pl.when(has_down)(lambda: layer_copy(x, 1).wait_recv())
        pl.when(has_up)(lambda: layer_copy(x, 0).wait_recv())

    def plane_wait(x):
        for k in ORDER:
            dx, dy = DIRECTIONS[k]
            pl.when(inside(-dx, -dy))(lambda: plane_copy(x, k).wait_recv())

    def halo_sent(x):
        for k in ORDER:
            pl.when(inside(*DIRECTIONS[k]))(lambda: plane_copy(x, k).wait_send())
        pl.when(has_up)(lambda: layer_copy(x, 1).wait_send())
        pl.when(has_down)(lambda: layer_copy(x, 0).wait_send())

    def apply(blocks, c, faces):
        weights = jnp.concatenate([tmpl[ids_ref[f, 0, c]] for f in faces], axis=0)
        return dot(jnp.concatenate(blocks, axis=1), weights)

    def own_pass(x):
        vector = vectors[x]

        @pl.loop(0, column_cap, unroll=UN_OWN)
        def _(c):
            blocks = [vector[c]]
            for q in range(4):
                r = refs_ref[q, c]
                blocks.append(vector[jnp.where((r < 0) | (r >= column_cap), zero_own, r)])
            acc[c] = apply(blocks, c, (0, 3, 4, 5, 6))

    def layer_pass(x):
        @pl.loop(0, column_cap, unroll=UN_LAYER)
        def _(c):
            acc[c] = acc[c] + apply([layers[x][0, c], layers[x][1, c]], c, (1, 2))

    def ghost_pass(x):
        @pl.loop(0, column_cap, unroll=UN_GHOST)
        def _(c):
            blocks = []
            for q in range(4):
                r = refs_ref[q, c]
                blocks.append(ghosts[x][jnp.where(r < column_cap, zero_ghost, r - column_cap)])
            total = acc[c] + apply(blocks, c, (3, 4, 5, 6))
            vectors[x + 1][c] = jnp.where(c < live, total, 0.0).astype(BF16)

    def gram(rows):
        def add(h, carry):
            pair = [
                jnp.concatenate([vectors[i][2 * h], vectors[i][2 * h + 1]], axis=1)
                for i in range(rows[-1] + 1)
            ]
            return tuple(
                total + dot_nt(pair[j], jnp.concatenate(pair[: j + 1], axis=0))
                for j, total in zip(rows, carry)
            )

        start = tuple(jnp.zeros((rhs, rhs * (j + 1)), F32) for j in rows)
        totals = lax.fori_loop(0, column_cap // 2, add, start, unroll=UN_GRAM)
        return [t[:, rhs * i : rhs * (i + 1)] for t in totals for i in range(t.shape[1] // rhs)]

    def mark(blocks):
        spare = [lists_ref[s, 0, k] for k in range(8) for s in range(caps[k], halo_cap)]
        if not spare:
            return blocks
        over = functools.reduce(jnp.maximum, spare) >= 0
        return [jnp.where(over, jnp.nan, blocks[0])] + blocks[1:]

    def pack(block):
        return jnp.concatenate([block[8 * i : 8 * i + 8] for i in range(rhs // 8)], axis=1)

    def unpack(line):
        return jnp.concatenate([line[:, rhs * i : rhs * (i + 1)] for i in range(rhs // 8)], axis=0)

    def send_all(w, hop, peers, place, source, slots, at):
        copies = [
            pltpu.make_async_remote_copy(
                src_ref=source,
                dst_ref=slots.at[at],
                send_sem=sum_send.at[w, hop, offset],
                recv_sem=sum_recv.at[w, hop, offset],
                device_id=place(offset),
                device_id_type=MESH,
            )
            for offset in range(1, peers)
        ]
        for copy in copies:
            copy.start()
        return copies

    def add_up(slots, peers):
        total = slots[0]
        for s in range(1, peers):
            total = total + slots[s]
        return total

    axes_z, axes_y, axes_x = (groups, on_z, g), (peers_y, on_y, at_y), (peers_x, on_x, me_x)

    def reduced(w, blocks):
        routes = ((axes_y, axes_z, axes_x), (axes_z, axes_y, axes_x))
        sums = [
            jnp.concatenate([pack(blocks[0]), pack(blocks[1])], axis=0),
            pack(blocks[2]),
        ]
        sent = []
        for hop in range(3):
            pending = []
            for way, total in enumerate(sums):
                peers, place, at = routes[way][hop]
                slots = (slots_a, slots_b)[way].at[w, hop]
                slots[at] = total
                copies = send_all(2 * w + way, hop, peers, place, slots.at[at], slots, at)
                pending.append((slots, peers, copies))
            yield None
            sums = []
            for slots, peers, copies in pending:
                for copy in copies:
                    copy.wait_recv()
                sent += copies
                sums.append(add_up(slots, peers))
        whole = [sums[0][:8], sums[0][8:], sums[1]]
        yield [unpack(line) * (1.0 / rows_total) for line in whole], sent

    lanes = work.shape[1]
    wide = lax.broadcasted_iota(jnp.int32, (rhs, lanes), 1)
    tall = lax.broadcasted_iota(jnp.int32, (rhs, lanes), 0)

    def factor(j, blocks):
        before = rhs * j
        corner = blocks[j]
        if j:
            left = exact_nt(jnp.concatenate(blocks[:j], axis=1), inv[:before, :before])
            corner = corner - exact_nt(left, left)
            across_inv = exact(left, inv[:before, :before])
        work[...] = jnp.where(wide == tall + rhs, 1.0, 0.0)
        work[:, :rhs] = corner
        m = work[...]
        for p in range(rhs // 8):
            size = rhs - 8 * p
            cols = [jnp.broadcast_to(m[:, 8 * p + i : 8 * p + i + 1], (size, lanes)) for i in range(8)]
            for i in range(8):
                scale = lax.rsqrt(jnp.broadcast_to(cols[i][i : i + 1, :], (size, lanes)))
                column = cols[i] * scale
                line = jnp.broadcast_to(m[i : i + 1, :], (size, lanes)) * scale
                upper[8 * p + i : 8 * p + i + 1, :] = line[0:1, :]
                m = m - column * line
                for n in range(i + 1, 8):
                    cols[n] = cols[n] - column * jnp.broadcast_to(column[n : n + 1, :], (size, lanes))
            m = m[8:]
        square = lax.broadcasted_iota(jnp.int32, (rhs, rhs), 0)
        across = lax.broadcasted_iota(jnp.int32, (rhs, rhs), 1)
        r_ref[before : before + rhs, before : before + rhs] = jnp.where(
            across >= square, upper[:, :rhs], 0.0
        )
        corner_inv = upper[:, rhs : 2 * rhs]
        inv[before : before + rhs, before : before + rhs] = corner_inv
        if j:
            r_ref[:before, before : before + rhs] = left.T
            r_ref[before : before + rhs, :before] = jnp.zeros((rhs, before), F32)
            inv[before : before + rhs, :before] = -exact(corner_inv, across_inv)

    def project(j):
        width = rhs * (j + 1)
        rows = inv[rhs * j : width, :width]
        high = rows.astype(BF16)
        low = (rows - high.astype(F32)).astype(BF16)
        both = jnp.concatenate([high, low], axis=1)

        @pl.loop(0, column_cap, unroll=UN_PROJ)
        def _(c):
            stack = [vectors[i][c] for i in range(j + 1)]
            q_ref[0, c, rhs * j : width, :] = dot(both, jnp.concatenate(stack + stack, axis=0)).astype(BF16)

    for k in ORDER:
        pack_packet(0, k)
    pl.semaphore_wait(barrier, expected)
    halo_start(0, True)
    load_templates.wait()

    @pl.loop(0, tmpl.shape[0], unroll=4)
    def _(t):
        tmpl[t] = tmpl[t].T

    own_pass(0)
    layers_wait(0)
    layer_pass(0)
    plane_wait(0)
    ghost_pass(0)

    halo_start(1, False)
    early = reduced(0, mark(gram((0, 1))))
    next(early)
    own_pass(1)
    layers_wait(1)
    layer_pass(1)
    next(early)
    plane_wait(1)
    ghost_pass(1)

    late = reduced(1, gram((2,)))
    next(late)
    next(early)
    next(late)
    (first, *second), sent_early = next(early)
    factor(0, [first])
    project(0)
    factor(1, second)
    next(late)
    project(1)
    third, sent_late = next(late)
    factor(2, third)
    project(2)
    halo_sent(0)
    halo_sent(1)
    for copy in sent_early + sent_late:
        copy.wait_send()


def solution(mesh):
    groups, pieces = mesh.shape["group"], mesh.shape["dom"]
    side = math.isqrt(pieces)
    peers_y = min(8, pieces // 2)
    peers_x = pieces // peers_y

    def body(basis_start, templates, template_ids, live_columns, face_refs, send_lists):
        _, column_cap, rhs, dof = basis_start.shape
        halo_cap = send_lists.shape[2]
        faces = template_ids.shape[2]
        width = 3 * rhs
        lanes = 128
        rows_total = column_cap * dof * groups * pieces
        vmem, smem = pltpu.VMEM, pltpu.SMEM
        block = (rhs, dof)
        operands = (
            basis_start,
            templates,
            template_ids.transpose(2, 0, 1),
            live_columns,
            face_refs.T,
            send_lists.transpose(2, 0, 1),
        )

        def run(caps, collective_id):
            return pl.pallas_call(
                functools.partial(kernel, groups, side, peers_y, rows_total, caps),
                out_shape=(
                    vmem((1, column_cap, width, dof), BF16),
                    vmem((width, width), F32),
                ),
                in_specs=[pl.BlockSpec(memory_space=pltpu.HBM)] * 6,
                out_specs=(pl.BlockSpec(memory_space=vmem), pl.BlockSpec(memory_space=vmem)),
                scratch_shapes=[
                    smem((faces, 1, column_cap), jnp.int32),
                    smem((1,), jnp.int32),
                    smem((4, column_cap), jnp.int32),
                    smem((halo_cap, 1, 8), jnp.int32),
                    vmem(templates.shape, BF16),
                    vmem((column_cap + 1, *block), BF16),
                    vmem((column_cap + 1, *block), BF16),
                    vmem((column_cap + 1, *block), BF16),
                    vmem((8 * halo_cap + 1, *block), BF16),
                    vmem((8 * halo_cap + 1, *block), BF16),
                    vmem((8, halo_cap, *block), BF16),
                    vmem((8, halo_cap, *block), BF16),
                    vmem((2, column_cap, *block), BF16),
                    vmem((2, column_cap, *block), BF16),
                    vmem((column_cap, *block), F32),
                    vmem((2, 3, 8, 16, lanes), F32),
                    vmem((2, 3, 8, 8, lanes), F32),
                    vmem((rhs, lanes), F32),
                    vmem((rhs, lanes), F32),
                    vmem((width, lanes), F32),
                    pltpu.SemaphoreType.DMA((6,)),
                    pltpu.SemaphoreType.DMA((2, 10)),
                    pltpu.SemaphoreType.DMA((2, 10)),
                    pltpu.SemaphoreType.DMA((4, 3, 8)),
                    pltpu.SemaphoreType.DMA((4, 3, 8)),
                ],
                compiler_params=pltpu.CompilerParams(
                    collective_id=collective_id, has_side_effects=True, vmem_limit_bytes=VMEM_MIB * 2**20
                ),
            )(*operands)

        narrow = [halo_cap if 0 in step else CORNER_CAP for step in DIRECTIONS]
        basis_q, r_factor = run(narrow, 0)
        return lax.cond(
            jnp.isnan(r_factor[0, 0]),
            lambda: tuple(run([halo_cap] * 8, 1)),
            lambda: (basis_q, r_factor),
        )

    return jax.shard_map(
        body,
        mesh=mesh,
        in_specs=(
            P("group", "dom", None, None),
            P(),
            P("group", "dom", None),
            P("dom"),
            P("dom", None),
            P("dom", None, None),
        ),
        out_specs=(P("group", "dom", None, None), P()),
        check_vma=False,
    )
```

```python
import functools
import math

import jax
import jax.numpy as jnp
from jax import lax
from jax.experimental import pallas as pl
from jax.experimental.pallas import tpu as pltpu
from jax.sharding import PartitionSpec as P

DIRECTIONS = ((-1, -1), (-1, 0), (-1, 1), (0, -1), (0, 1), (1, -1), (1, 0), (1, 1))
ORDER = (6, 1, 5, 7, 0, 2, 3, 4)
MESH = pl.DeviceIdType.MESH
F32 = jnp.float32
BF16 = jnp.bfloat16
NT = (((1,), (1,)), ((), ()))
HIGH = lax.Precision.HIGHEST
CORNER_CAP = 2
VMEM_MIB = 58
UN_OWN = UN_LAYER = UN_GHOST = UN_PROJ = 36
UN_GRAM = 18


def dot(x, y):
    return jnp.dot(x, y, preferred_element_type=F32)


def dot_nt(x, y):
    return lax.dot_general(x, y, NT, preferred_element_type=F32)


def exact(x, y):
    return jnp.dot(x, y, preferred_element_type=F32, precision=HIGH)


def exact_nt(x, y):
    return lax.dot_general(x, y, NT, preferred_element_type=F32, precision=HIGH)


def kernel(
    groups, side, peers_y, rows_total, caps,
    basis_ref, templates_ref, ids_in, live_in, refs_in, lists_in,
    q_ref, r_ref,
    ids_ref, live_ref, refs_ref, lists_ref, tmpl, v0, v1, v2, ghost1, ghost2, packet1, packet2, layer1, layer2, acc,
    slots_a, slots_b, work, upper, inv,
    load_sem, halo_send, halo_recv, sum_send, sum_recv,
):
    column_cap, rhs, dof = v0.shape[0] - 1, v0.shape[1], v0.shape[2]
    halo_cap = packet1.shape[1]
    zero_own, zero_ghost = column_cap, 8 * halo_cap
    vectors, ghosts, layers = (v0, v1, v2), (ghost1, ghost2), (layer1, layer2)
    packets = (packet1, packet2)
    pieces = side * side
    peers_x = pieces // peers_y
    g = lax.axis_index("group")
    d = lax.axis_index("dom")
    row, col = d // side, d % side
    core, at_y, at_x = d % 2, (d // 2) % peers_y, d // (2 * peers_y)
    me_x = at_x * 2 + core

    def on_z(offset):
        return ((g + offset) % groups, d)

    def on_y(offset):
        return (g, (at_x * peers_y + (at_y + offset) % peers_y) * 2 + core)

    def on_x(offset):
        other = (me_x + offset) % peers_x
        return (g, ((other // 2) * peers_y + at_y) * 2 + other % 2)

    def inside(dx, dy):
        return (row + dx >= 0) & (row + dx < side) & (col + dy >= 0) & (col + dy < side)

    barrier = pltpu.get_barrier_semaphore()

    def greet(device):
        pl.semaphore_signal(barrier, inc=1, device_id=device, device_id_type=MESH)

    expected = 0
    for dx, dy in (DIRECTIONS[k] for k in ORDER):
        target = (g, (row + dx) * side + col + dy)
        pl.when(inside(dx, dy))(functools.partial(greet, target))
        expected += inside(dx, dy).astype(jnp.int32)
    for peers, place in ((groups, on_z), (peers_y, on_y), (peers_x, on_x)):
        for offset in range(1, peers):
            greet(place(offset))
        expected += peers - 1

    loads = [
        pltpu.make_async_copy(source, target, load_sem.at[2 + i])
        for i, (source, target) in enumerate(
            ((lists_in, lists_ref), (live_in, live_ref), (ids_in, ids_ref), (refs_in, refs_ref))
        )
    ]
    for load in loads:
        load.start()
    load_templates = pltpu.make_async_copy(templates_ref, tmpl, load_sem.at[0])
    load_templates.start()
    load_basis = pltpu.make_async_copy(basis_ref.at[0], v0.at[pl.ds(0, column_cap)], load_sem.at[1])
    load_basis.start()

    empty = jnp.zeros((rhs, dof), BF16)
    for vector in vectors:
        vector[zero_own] = empty
    for x in range(2):
        ghosts[x][zero_ghost] = empty
        for k, (dx, dy) in enumerate(DIRECTIONS):
            @pl.when(jnp.logical_not(inside(-dx, -dy)))
            def _():
                ghosts[x][pl.ds(k * halo_cap, halo_cap)] = jnp.zeros((halo_cap, rhs, dof), BF16)

        @pl.when(g == 0)
        def _():
            layers[x][0] = jnp.zeros((column_cap, rhs, dof), BF16)

        @pl.when(g == groups - 1)
        def _():
            layers[x][1] = jnp.zeros((column_cap, rhs, dof), BF16)

    inv[...] = jnp.zeros(inv.shape, F32)
    for load in loads:
        load.wait()
    live = live_ref[0]
    load_basis.wait()

    @pl.loop(0, column_cap)
    def _(c):
        v0[c] = v0[c] * (c < live).astype(F32).astype(BF16)

    def plane_copy(x, k):
        dx, dy = DIRECTIONS[k]
        return pltpu.make_async_remote_copy(
            src_ref=packets[x].at[k, pl.ds(0, caps[k])],
            dst_ref=ghosts[x].at[pl.ds(k * halo_cap, caps[k])],
            send_sem=halo_send.at[x, k],
            recv_sem=halo_recv.at[x, k],
            device_id=(g, (row + dx) * side + col + dy),
            device_id_type=MESH,
        )

    def layer_copy(x, up):
        return pltpu.make_async_remote_copy(
            src_ref=vectors[x].at[pl.ds(0, column_cap)],
            dst_ref=layers[x].at[0 if up else 1],
            send_sem=halo_send.at[x, 8 + up],
            recv_sem=halo_recv.at[x, 8 + up],
            device_id=(g + 1 if up else g - 1, d),
            device_id_type=MESH,
        )

    has_up, has_down = g < groups - 1, g > 0

    def pack_packet(x, k):
        for s in range(caps[k]):
            slot = lists_ref[s, 0, k]
            packets[x][k, s] = vectors[x][jnp.where(slot < 0, zero_own, slot)]

    def layers_start(x):
        pl.when(has_up)(lambda: layer_copy(x, 1).start())
        pl.when(has_down)(lambda: layer_copy(x, 0).start())

    def plane_start(x, directions):
        for k in directions:
            pl.when(inside(*DIRECTIONS[k]))(lambda: plane_copy(x, k).start())

    def layers_wait(x):
        pl.when(has_down)(lambda: layer_copy(x, 1).wait_recv())
        pl.when(has_up)(lambda: layer_copy(x, 0).wait_recv())

    def plane_wait(x):
        for k in ORDER:
            dx, dy = DIRECTIONS[k]
            pl.when(inside(-dx, -dy))(lambda: plane_copy(x, k).wait_recv())

    def halo_sent(x):
        for k in ORDER:
            pl.when(inside(*DIRECTIONS[k]))(lambda: plane_copy(x, k).wait_send())
        pl.when(has_up)(lambda: layer_copy(x, 1).wait_send())
        pl.when(has_down)(lambda: layer_copy(x, 0).wait_send())

    def apply(blocks, c, faces):
        weights = jnp.concatenate([tmpl[ids_ref[f, 0, c]] for f in faces], axis=0)
        return dot(jnp.concatenate(blocks, axis=1), weights)

    def own_pass(x):
        vector = vectors[x]

        @pl.loop(0, column_cap, unroll=UN_OWN)
        def _(c):
            blocks = [vector[c]]
            for q in range(4):
                r = refs_ref[q, c]
                blocks.append(vector[jnp.where((r < 0) | (r >= column_cap), zero_own, r)])
            acc[c] = apply(blocks, c, (0, 3, 4, 5, 6))

    def layer_pass(x):
        @pl.loop(0, column_cap, unroll=UN_LAYER)
        def _(c):
            acc[c] = acc[c] + apply([layers[x][0, c], layers[x][1, c]], c, (1, 2))

    def finished(x, c):
        blocks = []
        for q in range(4):
            r = refs_ref[q, c]
            blocks.append(ghosts[x][jnp.where(r < column_cap, zero_ghost, r - column_cap)])
        return acc[c] + apply(blocks, c, (3, 4, 5, 6))

    def ghost_pass(x):
        @pl.loop(0, column_cap, unroll=UN_GHOST)
        def _(c):
            vectors[x + 1][c] = jnp.where(c < live, finished(x, c), 0.0).astype(BF16)

    def send_ahead(x):
        for k in ORDER[:6]:
            for s in range(caps[k]):
                slot = lists_ref[s, 0, k]
                c = jnp.maximum(slot, 0)
                keep = (slot >= 0) & (c < live)
                packets[x + 1][k, s] = jnp.where(keep, finished(x, c), 0.0).astype(BF16)
            pl.when(inside(*DIRECTIONS[k]))(lambda: plane_copy(x + 1, k).start())

    def ghost_pass_gram(x):
        def step(h, total):
            pair = []
            for c in (2 * h, 2 * h + 1):
                block = jnp.where(c < live, finished(x, c), 0.0).astype(BF16)
                vectors[x + 1][c] = block
                pair.append(block)
            lines = [jnp.concatenate([vectors[i][2 * h], vectors[i][2 * h + 1]], axis=1) for i in range(x + 1)]
            line = jnp.concatenate(pair, axis=1)
            return total + dot_nt(line, jnp.concatenate(lines + [line], axis=0))

        start = jnp.zeros((rhs, rhs * (x + 2)), F32)
        total = lax.fori_loop(0, column_cap // 2, step, start, unroll=UN_GRAM)
        return [total[:, rhs * i : rhs * (i + 1)] for i in range(x + 2)]

    def gram(rows):
        def add(h, carry):
            pair = [
                jnp.concatenate([vectors[i][2 * h], vectors[i][2 * h + 1]], axis=1)
                for i in range(rows[-1] + 1)
            ]
            return tuple(
                total + dot_nt(pair[j], jnp.concatenate(pair[: j + 1], axis=0))
                for j, total in zip(rows, carry)
            )

        start = tuple(jnp.zeros((rhs, rhs * (j + 1)), F32) for j in rows)
        totals = lax.fori_loop(0, column_cap // 2, add, start, unroll=UN_GRAM)
        return [t[:, rhs * i : rhs * (i + 1)] for t in totals for i in range(t.shape[1] // rhs)]

    def mark(blocks):
        spare = [lists_ref[s, 0, k] for k in range(8) for s in range(caps[k], halo_cap)]
        if not spare:
            return blocks
        over = functools.reduce(jnp.maximum, spare) >= 0
        return [jnp.where(over, jnp.nan, blocks[0])] + blocks[1:]

    def pack(block):
        return jnp.concatenate([block[8 * i : 8 * i + 8] for i in range(rhs // 8)], axis=1)

    def unpack(line):
        return jnp.concatenate([line[:, rhs * i : rhs * (i + 1)] for i in range(rhs // 8)], axis=0)

    def send_all(w, hop, peers, place, source, slots, at):
        copies = [
            pltpu.make_async_remote_copy(
                src_ref=source,
                dst_ref=slots.at[at],
                send_sem=sum_send.at[w, hop, offset],
                recv_sem=sum_recv.at[w, hop, offset],
                device_id=place(offset),
                device_id_type=MESH,
            )
            for offset in range(1, peers)
        ]
        for copy in copies:
            copy.start()
        return copies

    def add_up(slots, peers):
        total = slots[0]
        for s in range(1, peers):
            total = total + slots[s]
        return total

    axes_z, axes_y, axes_x = (groups, on_z, g), (peers_y, on_y, at_y), (peers_x, on_x, me_x)

    def reduced(w, blocks):
        routes = ((axes_y, axes_z, axes_x), (axes_z, axes_y, axes_x))
        sums = [
            jnp.concatenate([pack(blocks[0]), pack(blocks[1])], axis=0),
            pack(blocks[2]),
        ]
        sent = []
        for hop in range(3):
            pending = []
            for way, total in enumerate(sums):
                peers, place, at = routes[way][hop]
                slots = (slots_a, slots_b)[way].at[w, hop]
                slots[at] = total
                copies = send_all(2 * w + way, hop, peers, place, slots.at[at], slots, at)
                pending.append((slots, peers, copies))
            yield None
            sums = []
            for slots, peers, copies in pending:
                for copy in copies:
                    copy.wait_recv()
                sent += copies
                sums.append(add_up(slots, peers))
        whole = [sums[0][:8], sums[0][8:], sums[1]]
        yield [unpack(line) * (1.0 / rows_total) for line in whole], sent

    lanes = work.shape[1]
    wide = lax.broadcasted_iota(jnp.int32, (rhs, lanes), 1)
    tall = lax.broadcasted_iota(jnp.int32, (rhs, lanes), 0)

    def factor(j, blocks):
        before = rhs * j
        corner = blocks[j]
        if j:
            left = exact_nt(jnp.concatenate(blocks[:j], axis=1), inv[:before, :before])
            corner = corner - exact_nt(left, left)
            across_inv = exact(left, inv[:before, :before])
        work[...] = jnp.where(wide == tall + rhs, 1.0, 0.0)
        work[:, :rhs] = corner
        m = work[...]
        for p in range(rhs // 8):
            size = rhs - 8 * p
            cols = [jnp.broadcast_to(m[:, 8 * p + i : 8 * p + i + 1], (size, lanes)) for i in range(8)]
            for i in range(8):
                scale = lax.rsqrt(jnp.broadcast_to(cols[i][i : i + 1, :], (size, lanes)))
                column = cols[i] * scale
                line = jnp.broadcast_to(m[i : i + 1, :], (size, lanes)) * scale
                upper[8 * p + i : 8 * p + i + 1, :] = line[0:1, :]
                m = m - column * line
                for n in range(i + 1, 8):
                    cols[n] = cols[n] - column * jnp.broadcast_to(column[n : n + 1, :], (size, lanes))
            m = m[8:]
        square = lax.broadcasted_iota(jnp.int32, (rhs, rhs), 0)
        across = lax.broadcasted_iota(jnp.int32, (rhs, rhs), 1)
        r_ref[before : before + rhs, before : before + rhs] = jnp.where(
            across >= square, upper[:, :rhs], 0.0
        )
        corner_inv = upper[:, rhs : 2 * rhs]
        inv[before : before + rhs, before : before + rhs] = corner_inv
        if j:
            r_ref[:before, before : before + rhs] = left.T
            r_ref[before : before + rhs, :before] = jnp.zeros((rhs, before), F32)
            inv[before : before + rhs, :before] = -exact(corner_inv, across_inv)

    def project(j):
        width = rhs * (j + 1)
        rows = inv[rhs * j : width, :width]
        high = rows.astype(BF16)
        low = (rows - high.astype(F32)).astype(BF16)
        both = jnp.concatenate([high, low], axis=1)

        @pl.loop(0, column_cap, unroll=UN_PROJ)
        def _(c):
            stack = [vectors[i][c] for i in range(j + 1)]
            q_ref[0, c, rhs * j : width, :] = dot(both, jnp.concatenate(stack + stack, axis=0)).astype(BF16)

    for k in ORDER:
        pack_packet(0, k)
    pl.semaphore_wait(barrier, expected)
    plane_start(0, ORDER[:6])
    layers_start(0)
    plane_start(0, ORDER[6:])
    load_templates.wait()

    @pl.loop(0, tmpl.shape[0], unroll=4)
    def _(t):
        tmpl[t] = tmpl[t].T

    own_pass(0)
    layers_wait(0)
    layer_pass(0)
    plane_wait(0)
    send_ahead(0)
    ghost_pass(0)

    layers_start(1)
    for k in ORDER[6:]:
        pack_packet(1, k)
    plane_start(1, ORDER[6:])
    early = reduced(0, mark(gram((0, 1))))
    next(early)
    own_pass(1)
    layers_wait(1)
    layer_pass(1)
    next(early)
    plane_wait(1)
    late = reduced(1, ghost_pass_gram(1))
    next(late)
    next(early)
    next(late)
    (first, *second), sent_early = next(early)
    factor(0, [first])
    project(0)
    factor(1, second)
    next(late)
    project(1)
    third, sent_late = next(late)
    factor(2, third)
    project(2)
    halo_sent(0)
    halo_sent(1)
    for copy in sent_early + sent_late:
        copy.wait_send()


def solution(mesh):
    groups, pieces = mesh.shape["group"], mesh.shape["dom"]
    side = math.isqrt(pieces)
    peers_y = min(8, pieces // 2)
    peers_x = pieces // peers_y

    def body(basis_start, templates, template_ids, live_columns, face_refs, send_lists):
        _, column_cap, rhs, dof = basis_start.shape
        halo_cap = send_lists.shape[2]
        faces = template_ids.shape[2]
        width = 3 * rhs
        lanes = 128
        rows_total = column_cap * dof * groups * pieces
        vmem, smem = pltpu.VMEM, pltpu.SMEM
        block = (rhs, dof)
        operands = (
            basis_start,
            templates,
            template_ids.transpose(2, 0, 1),
            live_columns,
            face_refs.T,
            send_lists.transpose(2, 0, 1),
        )

        def run(caps, collective_id):
            return pl.pallas_call(
                functools.partial(kernel, groups, side, peers_y, rows_total, caps),
                out_shape=(
                    vmem((1, column_cap, width, dof), BF16),
                    vmem((width, width), F32),
                ),
                in_specs=[pl.BlockSpec(memory_space=pltpu.HBM)] * 6,
                out_specs=(pl.BlockSpec(memory_space=vmem), pl.BlockSpec(memory_space=vmem)),
                scratch_shapes=[
                    smem((faces, 1, column_cap), jnp.int32),
                    smem((1,), jnp.int32),
                    smem((4, column_cap), jnp.int32),
                    smem((halo_cap, 1, 8), jnp.int32),
                    vmem(templates.shape, BF16),
                    vmem((column_cap + 1, *block), BF16),
                    vmem((column_cap + 1, *block), BF16),
                    vmem((column_cap + 1, *block), BF16),
                    vmem((8 * halo_cap + 1, *block), BF16),
                    vmem((8 * halo_cap + 1, *block), BF16),
                    vmem((8, halo_cap, *block), BF16),
                    vmem((8, halo_cap, *block), BF16),
                    vmem((2, column_cap, *block), BF16),
                    vmem((2, column_cap, *block), BF16),
                    vmem((column_cap, *block), F32),
                    vmem((2, 3, 8, 16, lanes), F32),
                    vmem((2, 3, 8, 8, lanes), F32),
                    vmem((rhs, lanes), F32),
                    vmem((rhs, lanes), F32),
                    vmem((width, lanes), F32),
                    pltpu.SemaphoreType.DMA((6,)),
                    pltpu.SemaphoreType.DMA((2, 10)),
                    pltpu.SemaphoreType.DMA((2, 10)),
                    pltpu.SemaphoreType.DMA((4, 3, 8)),
                    pltpu.SemaphoreType.DMA((4, 3, 8)),
                ],
                compiler_params=pltpu.CompilerParams(
                    collective_id=collective_id, has_side_effects=True, vmem_limit_bytes=VMEM_MIB * 2**20
                ),
            )(*operands)

        narrow = [halo_cap if 0 in step else CORNER_CAP for step in DIRECTIONS]
        basis_q, r_factor = run(narrow, 0)
        return lax.cond(
            jnp.isnan(r_factor[0, 0]),
            lambda: tuple(run([halo_cap] * 8, 1)),
            lambda: (basis_q, r_factor),
        )

    return jax.shard_map(
        body,
        mesh=mesh,
        in_specs=(
            P("group", "dom", None, None),
            P(),
            P("group", "dom", None),
            P("dom"),
            P("dom", None),
            P("dom", None, None),
        ),
        out_specs=(P("group", "dom", None, None), P()),
        check_vma=False,
    )
```

```python
import functools
import math

import jax
import jax.numpy as jnp
from jax import lax
from jax.experimental import pallas as pl
from jax.experimental.pallas import tpu as pltpu
from jax.sharding import PartitionSpec as P

DIRECTIONS = ((-1, -1), (-1, 0), (-1, 1), (0, -1), (0, 1), (1, -1), (1, 0), (1, 1))
ORDER = (6, 1, 5, 7, 0, 2, 3, 4)
MESH = pl.DeviceIdType.MESH
F32 = jnp.float32
BF16 = jnp.bfloat16
NT = (((1,), (1,)), ((), ()))
HIGH = lax.Precision.HIGHEST
CORNER_CAP = 2
VMEM_MIB = 56
LAST_MIB = 24
UN_OWN = UN_LAYER = UN_GHOST = UN_PROJ = 36
UN_GRAM = 18


def dot(x, y):
    return jnp.dot(x, y, preferred_element_type=F32)


def dot_nt(x, y):
    return lax.dot_general(x, y, NT, preferred_element_type=F32)


def exact(x, y):
    return jnp.dot(x, y, preferred_element_type=F32, precision=HIGH)


def exact_nt(x, y):
    return lax.dot_general(x, y, NT, preferred_element_type=F32, precision=HIGH)


def factor(j, blocks, inv, work, upper, r_ref):
    rhs, lanes = work.shape
    before = rhs * j
    wide = lax.broadcasted_iota(jnp.int32, (rhs, lanes), 1)
    tall = lax.broadcasted_iota(jnp.int32, (rhs, lanes), 0)
    corner = blocks[j]
    if j:
        left = exact_nt(jnp.concatenate(blocks[:j], axis=1), inv[:before, :before])
        corner = corner - exact_nt(left, left)
        across_inv = exact(left, inv[:before, :before])
    work[...] = jnp.where(wide == tall + rhs, 1.0, 0.0)
    work[:, :rhs] = corner
    m = work[...]
    for p in range(rhs // 8):
        size = rhs - 8 * p
        cols = [jnp.broadcast_to(m[:, 8 * p + i : 8 * p + i + 1], (size, lanes)) for i in range(8)]
        for i in range(8):
            scale = lax.rsqrt(jnp.broadcast_to(cols[i][i : i + 1, :], (size, lanes)))
            column = cols[i] * scale
            line = jnp.broadcast_to(m[i : i + 1, :], (size, lanes)) * scale
            upper[8 * p + i : 8 * p + i + 1, :] = line[0:1, :]
            m = m - column * line
            for n in range(i + 1, 8):
                cols[n] = cols[n] - column * jnp.broadcast_to(column[n : n + 1, :], (size, lanes))
        m = m[8:]
    square = lax.broadcasted_iota(jnp.int32, (rhs, rhs), 0)
    across = lax.broadcasted_iota(jnp.int32, (rhs, rhs), 1)
    r_ref[before : before + rhs, before : before + rhs] = jnp.where(
        across >= square, upper[:, :rhs], 0.0
    )
    corner_inv = upper[:, rhs : 2 * rhs]
    inv[before : before + rhs, before : before + rhs] = corner_inv
    if j:
        r_ref[:before, before : before + rhs] = left.T
        r_ref[before : before + rhs, :before] = jnp.zeros((rhs, before), F32)
        inv[before : before + rhs, :before] = -exact(corner_inv, across_inv)


def project(j, vectors, inv, put):
    column_cap, rhs = vectors[0].shape[0] - 1, vectors[0].shape[1]
    width = rhs * (j + 1)
    rows = inv[rhs * j : width, :width]
    high = rows.astype(BF16)
    low = (rows - high.astype(F32)).astype(BF16)
    both = jnp.concatenate([high, low], axis=1)
    for c in range(column_cap):
        stack = [vectors[i][c] for i in range(j + 1)]
        put(c, dot(both, jnp.concatenate(stack + stack, axis=0)).astype(BF16))


def last_kernel(
    v0, v1, v2, early_q, early_inv, early_r, lines_ref,
    q_ref, r_ref,
    inv, work, upper, late_q, sems,
):
    column_cap, rhs, _ = late_q.shape
    early_copy = pltpu.make_async_copy(early_q, q_ref.at[0, :, pl.ds(0, 2 * rhs)], sems.at[0])
    early_copy.start()
    inv[...] = early_inv[...]
    r_ref[...] = early_r[...]
    lines = lines_ref[...]
    factor(2, [lines[:, rhs * i : rhs * (i + 1)] for i in range(3)], inv, work, upper, r_ref)
    part = column_cap // 3
    copies = [
        pltpu.make_async_copy(
            late_q.at[pl.ds(part * i, part)],
            q_ref.at[0, pl.ds(part * i, part), pl.ds(2 * rhs, rhs)],
            sems.at[1 + i],
        )
        for i in range(3)
    ]

    def put(c, block):
        late_q[c] = block
        if (c + 1) % part == 0:
            copies[c // part].start()

    project(2, (v0, v1, v2), inv, put)
    early_copy.wait()
    for copy in copies:
        copy.wait()


def kernel(
    groups, side, peers_y, rows_total, caps,
    basis_ref, templates_ref, ids_in, live_in, refs_in, lists_in,
    v0, v1, v2, early_q, inv, r_ref, lines_ref, over_ref,
    ids_ref, live_ref, refs_ref, lists_ref, tmpl, ghost1, ghost2, packet1, packet2, layer1, layer2, acc,
    slots_a, slots_b, work, upper,
    load_sem, halo_send, halo_recv, sum_send, sum_recv,
):
    column_cap, rhs, dof = v0.shape[0] - 1, v0.shape[1], v0.shape[2]
    halo_cap = packet1.shape[1]
    zero_own, zero_ghost = column_cap, 8 * halo_cap
    vectors, ghosts, layers = (v0, v1, v2), (ghost1, ghost2), (layer1, layer2)
    packets = (packet1, packet2)
    pieces = side * side
    peers_x = pieces // peers_y
    g = lax.axis_index("group")
    d = lax.axis_index("dom")
    row, col = d // side, d % side
    core, at_y, at_x = d % 2, (d // 2) % peers_y, d // (2 * peers_y)
    me_x = at_x * 2 + core

    def on_z(offset):
        return ((g + offset) % groups, d)

    def on_y(offset):
        return (g, (at_x * peers_y + (at_y + offset) % peers_y) * 2 + core)

    def on_x(offset):
        other = (me_x + offset) % peers_x
        return (g, ((other // 2) * peers_y + at_y) * 2 + other % 2)

    def inside(dx, dy):
        return (row + dx >= 0) & (row + dx < side) & (col + dy >= 0) & (col + dy < side)

    barrier = pltpu.get_barrier_semaphore()

    def greet(device):
        pl.semaphore_signal(barrier, inc=1, device_id=device, device_id_type=MESH)

    expected = 0
    for dx, dy in (DIRECTIONS[k] for k in ORDER):
        target = (g, (row + dx) * side + col + dy)
        pl.when(inside(dx, dy))(functools.partial(greet, target))
        expected += inside(dx, dy).astype(jnp.int32)
    for peers, place in ((groups, on_z), (peers_y, on_y), (peers_x, on_x)):
        for offset in range(1, peers):
            greet(place(offset))
        expected += peers - 1

    loads = [
        pltpu.make_async_copy(source, target, load_sem.at[2 + i])
        for i, (source, target) in enumerate(
            ((lists_in, lists_ref), (live_in, live_ref), (ids_in, ids_ref), (refs_in, refs_ref))
        )
    ]
    for load in loads:
        load.start()
    load_templates = pltpu.make_async_copy(templates_ref, tmpl, load_sem.at[0])
    load_templates.start()
    load_basis = pltpu.make_async_copy(basis_ref.at[0], v0.at[pl.ds(0, column_cap)], load_sem.at[1])
    load_basis.start()

    empty = jnp.zeros((rhs, dof), BF16)
    for vector in vectors:
        vector[zero_own] = empty
    for x in range(2):
        ghosts[x][zero_ghost] = empty
        for k, (dx, dy) in enumerate(DIRECTIONS):
            @pl.when(jnp.logical_not(inside(-dx, -dy)))
            def _():
                ghosts[x][pl.ds(k * halo_cap, halo_cap)] = jnp.zeros((halo_cap, rhs, dof), BF16)

        @pl.when(g == 0)
        def _():
            layers[x][0] = jnp.zeros((column_cap, rhs, dof), BF16)

        @pl.when(g == groups - 1)
        def _():
            layers[x][1] = jnp.zeros((column_cap, rhs, dof), BF16)

    inv[...] = jnp.zeros(inv.shape, F32)
    r_ref[...] = jnp.zeros(r_ref.shape, F32)
    for load in loads:
        load.wait()
    live = live_ref[0]
    load_basis.wait()

    @pl.loop(0, column_cap)
    def _(c):
        v0[c] = v0[c] * (c < live).astype(F32).astype(BF16)

    def plane_copy(x, k):
        dx, dy = DIRECTIONS[k]
        return pltpu.make_async_remote_copy(
            src_ref=packets[x].at[k, pl.ds(0, caps[k])],
            dst_ref=ghosts[x].at[pl.ds(k * halo_cap, caps[k])],
            send_sem=halo_send.at[x, k],
            recv_sem=halo_recv.at[x, k],
            device_id=(g, (row + dx) * side + col + dy),
            device_id_type=MESH,
        )

    def layer_copy(x, up):
        return pltpu.make_async_remote_copy(
            src_ref=vectors[x].at[pl.ds(0, column_cap)],
            dst_ref=layers[x].at[0 if up else 1],
            send_sem=halo_send.at[x, 8 + up],
            recv_sem=halo_recv.at[x, 8 + up],
            device_id=(g + 1 if up else g - 1, d),
            device_id_type=MESH,
        )

    has_up, has_down = g < groups - 1, g > 0

    def pack_packet(x, k):
        for s in range(caps[k]):
            slot = lists_ref[s, 0, k]
            packets[x][k, s] = vectors[x][jnp.where(slot < 0, zero_own, slot)]

    def halo_start(x, packed):
        for k in ORDER:
            if k == 3:
                pl.when(has_up)(lambda: layer_copy(x, 1).start())
                pl.when(has_down)(lambda: layer_copy(x, 0).start())
            if not packed:
                pack_packet(x, k)
            pl.when(inside(*DIRECTIONS[k]))(lambda: plane_copy(x, k).start())

    def layers_wait(x):
        pl.when(has_down)(lambda: layer_copy(x, 1).wait_recv())
        pl.when(has_up)(lambda: layer_copy(x, 0).wait_recv())

    def plane_wait(x):
        for k in ORDER:
            dx, dy = DIRECTIONS[k]
            pl.when(inside(-dx, -dy))(lambda: plane_copy(x, k).wait_recv())

    def halo_sent(x):
        for k in ORDER:
            pl.when(inside(*DIRECTIONS[k]))(lambda: plane_copy(x, k).wait_send())
        pl.when(has_up)(lambda: layer_copy(x, 1).wait_send())
        pl.when(has_down)(lambda: layer_copy(x, 0).wait_send())

    def apply(blocks, c, faces):
        weights = jnp.concatenate([tmpl[ids_ref[f, 0, c]] for f in faces], axis=0)
        return dot(jnp.concatenate(blocks, axis=1), weights)

    def own_pass(x):
        vector = vectors[x]

        @pl.loop(0, column_cap, unroll=UN_OWN)
        def _(c):
            blocks = [vector[c]]
            for q in range(4):
                r = refs_ref[q, c]
                blocks.append(vector[jnp.where((r < 0) | (r >= column_cap), zero_own, r)])
            acc[c] = apply(blocks, c, (0, 3, 4, 5, 6))

    def layer_pass(x):
        @pl.loop(0, column_cap, unroll=UN_LAYER)
        def _(c):
            acc[c] = acc[c] + apply([layers[x][0, c], layers[x][1, c]], c, (1, 2))

    def ghost_pass(x):
        @pl.loop(0, column_cap, unroll=UN_GHOST)
        def _(c):
            blocks = []
            for q in range(4):
                r = refs_ref[q, c]
                blocks.append(ghosts[x][jnp.where(r < column_cap, zero_ghost, r - column_cap)])
            total = acc[c] + apply(blocks, c, (3, 4, 5, 6))
            vectors[x + 1][c] = jnp.where(c < live, total, 0.0).astype(BF16)

    def gram(rows):
        def add(h, carry):
            pair = [
                jnp.concatenate([vectors[i][2 * h], vectors[i][2 * h + 1]], axis=1)
                for i in range(rows[-1] + 1)
            ]
            return tuple(
                total + dot_nt(pair[j], jnp.concatenate(pair[: j + 1], axis=0))
                for j, total in zip(rows, carry)
            )

        start = tuple(jnp.zeros((rhs, rhs * (j + 1)), F32) for j in rows)
        totals = lax.fori_loop(0, column_cap // 2, add, start, unroll=UN_GRAM)
        return [t[:, rhs * i : rhs * (i + 1)] for t in totals for i in range(t.shape[1] // rhs)]

    def mark(blocks):
        spare = [lists_ref[s, 0, k] for k in range(8) for s in range(caps[k], halo_cap)]
        if not spare:
            return blocks
        over = functools.reduce(jnp.maximum, spare) >= 0
        return [jnp.where(over, jnp.nan, blocks[0])] + blocks[1:]

    def pack(block):
        return jnp.concatenate([block[8 * i : 8 * i + 8] for i in range(rhs // 8)], axis=1)

    def unpack(line):
        return jnp.concatenate([line[:, rhs * i : rhs * (i + 1)] for i in range(rhs // 8)], axis=0)

    def send_all(w, hop, peers, place, source, slots, at):
        copies = [
            pltpu.make_async_remote_copy(
                src_ref=source,
                dst_ref=slots.at[at],
                send_sem=sum_send.at[w, hop, offset],
                recv_sem=sum_recv.at[w, hop, offset],
                device_id=place(offset),
                device_id_type=MESH,
            )
            for offset in range(1, peers)
        ]
        for copy in copies:
            copy.start()
        return copies

    def add_up(slots, peers):
        total = slots[0]
        for s in range(1, peers):
            total = total + slots[s]
        return total

    axes_z, axes_y, axes_x = (groups, on_z, g), (peers_y, on_y, at_y), (peers_x, on_x, me_x)

    def reduced(w, blocks):
        routes = ((axes_y, axes_z, axes_x), (axes_z, axes_y, axes_x))
        sums = [
            jnp.concatenate([pack(blocks[0]), pack(blocks[1])], axis=0),
            pack(blocks[2]),
        ]
        sent = []
        for hop in range(3):
            pending = []
            for way, total in enumerate(sums):
                peers, place, at = routes[way][hop]
                slots = (slots_a, slots_b)[way].at[w, hop]
                slots[at] = total
                copies = send_all(2 * w + way, hop, peers, place, slots.at[at], slots, at)
                pending.append((slots, peers, copies))
            yield None
            sums = []
            for slots, peers, copies in pending:
                for copy in copies:
                    copy.wait_recv()
                sent += copies
                sums.append(add_up(slots, peers))
        whole = [sums[0][:8], sums[0][8:], sums[1]]
        yield [unpack(line) * (1.0 / rows_total) for line in whole], sent

    for k in ORDER:
        pack_packet(0, k)
    pl.semaphore_wait(barrier, expected)
    halo_start(0, True)
    load_templates.wait()

    @pl.loop(0, tmpl.shape[0], unroll=4)
    def _(t):
        tmpl[t] = tmpl[t].T

    own_pass(0)
    layers_wait(0)
    layer_pass(0)
    plane_wait(0)
    ghost_pass(0)

    halo_start(1, False)
    early = reduced(0, mark(gram((0, 1))))
    next(early)
    own_pass(1)
    layers_wait(1)
    layer_pass(1)
    next(early)
    plane_wait(1)
    ghost_pass(1)

    late = reduced(1, gram((2,)))
    next(late)
    next(early)
    next(late)
    (first, *second), sent_early = next(early)
    over_ref[0] = jnp.max(jnp.where(first == first, 0, 1))

    def put_at(j):
        def put(c, block):
            early_q[c, rhs * j : rhs * (j + 1), :] = block

        return put

    factor(0, [first], inv, work, upper, r_ref)
    project(0, vectors, inv, put_at(0))
    factor(1, second, inv, work, upper, r_ref)
    next(late)
    project(1, vectors, inv, put_at(1))
    third, sent_late = next(late)
    lines_ref[...] = jnp.concatenate(third, axis=1)
    halo_sent(0)
    halo_sent(1)
    for copy in sent_early + sent_late:
        copy.wait_send()


def solution(mesh):
    groups, pieces = mesh.shape["group"], mesh.shape["dom"]
    side = math.isqrt(pieces)
    peers_y = min(8, pieces // 2)
    peers_x = pieces // peers_y

    def body(basis_start, templates, template_ids, live_columns, face_refs, send_lists):
        _, column_cap, rhs, dof = basis_start.shape
        halo_cap = send_lists.shape[2]
        faces = template_ids.shape[2]
        width = 3 * rhs
        lanes = 128
        rows_total = column_cap * dof * groups * pieces
        vmem, smem = pltpu.VMEM, pltpu.SMEM
        block = (rhs, dof)
        operands = (
            basis_start,
            templates,
            template_ids.transpose(2, 0, 1),
            live_columns,
            face_refs.T,
            send_lists.transpose(2, 0, 1),
        )

        def run(caps, collective_id):
            *early, over = pl.pallas_call(
                functools.partial(kernel, groups, side, peers_y, rows_total, caps),
                out_shape=(
                    vmem((column_cap + 1, *block), BF16),
                    vmem((column_cap + 1, *block), BF16),
                    vmem((column_cap + 1, *block), BF16),
                    vmem((column_cap, 2 * rhs, dof), BF16),
                    vmem((width, lanes), F32),
                    vmem((width, width), F32),
                    vmem((rhs, width), F32),
                    smem((1,), jnp.int32),
                ),
                in_specs=[pl.BlockSpec(memory_space=pltpu.HBM)] * 6,
                out_specs=tuple([pl.BlockSpec(memory_space=vmem)] * 7 + [pl.BlockSpec(memory_space=smem)]),
                scratch_shapes=[
                    smem((faces, 1, column_cap), jnp.int32),
                    smem((1,), jnp.int32),
                    smem((4, column_cap), jnp.int32),
                    smem((halo_cap, 1, 8), jnp.int32),
                    vmem(templates.shape, BF16),
                    vmem((8 * halo_cap + 1, *block), BF16),
                    vmem((8 * halo_cap + 1, *block), BF16),
                    vmem((8, halo_cap, *block), BF16),
                    vmem((8, halo_cap, *block), BF16),
                    vmem((2, column_cap, *block), BF16),
                    vmem((2, column_cap, *block), BF16),
                    vmem((column_cap, *block), F32),
                    vmem((2, 3, 8, 16, lanes), F32),
                    vmem((2, 3, 8, 8, lanes), F32),
                    vmem((rhs, lanes), F32),
                    vmem((rhs, lanes), F32),
                    pltpu.SemaphoreType.DMA((6,)),
                    pltpu.SemaphoreType.DMA((2, 10)),
                    pltpu.SemaphoreType.DMA((2, 10)),
                    pltpu.SemaphoreType.DMA((4, 3, 8)),
                    pltpu.SemaphoreType.DMA((4, 3, 8)),
                ],
                compiler_params=pltpu.CompilerParams(
                    collective_id=collective_id, has_side_effects=True, vmem_limit_bytes=VMEM_MIB * 2**20
                ),
            )(*operands)

            basis_q, r_factor = pl.pallas_call(
                last_kernel,
                out_shape=(
                    jax.ShapeDtypeStruct((1, column_cap, width, dof), BF16),
                    jax.ShapeDtypeStruct((width, width), F32),
                ),
                in_specs=[pl.BlockSpec(memory_space=vmem)] * 7,
                out_specs=(pl.BlockSpec(memory_space=pltpu.HBM), pl.BlockSpec(memory_space=vmem)),
                scratch_shapes=[
                    vmem((width, lanes), F32),
                    vmem((rhs, lanes), F32),
                    vmem((rhs, lanes), F32),
                    vmem((column_cap, *block), BF16),
                    pltpu.SemaphoreType.DMA((4,)),
                ],
                compiler_params=pltpu.CompilerParams(vmem_limit_bytes=LAST_MIB * 2**20),
            )(*early)
            return basis_q, r_factor, over

        narrow = [halo_cap if 0 in step else CORNER_CAP for step in DIRECTIONS]
        basis_q, r_factor, over = run(narrow, 0)
        return lax.cond(
            over[0] != 0,
            lambda: tuple(run([halo_cap] * 8, 1)[:2]),
            lambda: (basis_q, r_factor),
        )

    return jax.shard_map(
        body,
        mesh=mesh,
        in_specs=(
            P("group", "dom", None, None),
            P(),
            P("group", "dom", None),
            P("dom"),
            P("dom", None),
            P("dom", None, None),
        ),
        out_specs=(P("group", "dom", None, None), P()),
        check_vma=False,
    )
```

```python
import functools
import math

import jax
import jax.numpy as jnp
from jax import lax
from jax.experimental import pallas as pl
from jax.experimental.pallas import tpu as pltpu
from jax.sharding import PartitionSpec as P

DIRECTIONS = ((-1, -1), (-1, 0), (-1, 1), (0, -1), (0, 1), (1, -1), (1, 0), (1, 1))
ORDER = (6, 1, 5, 7, 0, 2, 3, 4)
MESH = pl.DeviceIdType.MESH
F32 = jnp.float32
BF16 = jnp.bfloat16
NT = (((1,), (1,)), ((), ()))
HIGH = lax.Precision.HIGHEST
CORNER_CAP = 2
VMEM_MIB = 56
LAST_MIB = 24
UN_OWN = UN_LAYER = UN_GHOST = UN_PROJ = 36
UN_GRAM = 18


def dot(x, y):
    return jnp.dot(x, y, preferred_element_type=F32)


def dot_nt(x, y):
    return lax.dot_general(x, y, NT, preferred_element_type=F32)


def exact(x, y):
    return jnp.dot(x, y, preferred_element_type=F32, precision=HIGH)


def exact_nt(x, y):
    return lax.dot_general(x, y, NT, preferred_element_type=F32, precision=HIGH)


def factor(j, blocks, inv, work, upper, r_ref):
    rhs, lanes = work.shape
    before = rhs * j
    wide = lax.broadcasted_iota(jnp.int32, (rhs, lanes), 1)
    tall = lax.broadcasted_iota(jnp.int32, (rhs, lanes), 0)
    corner = blocks[j]
    if j:
        left = exact_nt(jnp.concatenate(blocks[:j], axis=1), inv[:before, :before])
        corner = corner - exact_nt(left, left)
        across_inv = exact(left, inv[:before, :before])
    work[...] = jnp.where(wide == tall + rhs, 1.0, 0.0)
    work[:, :rhs] = corner
    m = work[...]
    for p in range(rhs // 8):
        size = rhs - 8 * p
        cols = [jnp.broadcast_to(m[:, 8 * p + i : 8 * p + i + 1], (size, lanes)) for i in range(8)]
        for i in range(8):
            scale = lax.rsqrt(jnp.broadcast_to(cols[i][i : i + 1, :], (size, lanes)))
            column = cols[i] * scale
            line = jnp.broadcast_to(m[i : i + 1, :], (size, lanes)) * scale
            upper[8 * p + i : 8 * p + i + 1, :] = line[0:1, :]
            m = m - column * line
            for n in range(i + 1, 8):
                cols[n] = cols[n] - column * jnp.broadcast_to(column[n : n + 1, :], (size, lanes))
        m = m[8:]
    square = lax.broadcasted_iota(jnp.int32, (rhs, rhs), 0)
    across = lax.broadcasted_iota(jnp.int32, (rhs, rhs), 1)
    r_ref[before : before + rhs, before : before + rhs] = jnp.where(
        across >= square, upper[:, :rhs], 0.0
    )
    corner_inv = upper[:, rhs : 2 * rhs]
    inv[before : before + rhs, before : before + rhs] = corner_inv
    if j:
        r_ref[:before, before : before + rhs] = left.T
        r_ref[before : before + rhs, :before] = jnp.zeros((rhs, before), F32)
        inv[before : before + rhs, :before] = -exact(corner_inv, across_inv)


def project(j, vectors, inv, put):
    column_cap, rhs = vectors[0].shape[0] - 1, vectors[0].shape[1]
    width = rhs * (j + 1)
    rows = inv[rhs * j : width, :width]
    high = rows.astype(BF16)
    low = (rows - high.astype(F32)).astype(BF16)
    both = jnp.concatenate([high, low], axis=1)
    for c in range(column_cap):
        stack = [vectors[i][c] for i in range(j + 1)]
        put(c, dot(both, jnp.concatenate(stack + stack, axis=0)).astype(BF16))


def last_kernel(
    v0, v1, v2, early_q, early_inv, early_r, lines_ref,
    q_ref, r_out,
    inv, work, upper, late_q, r_ref, sems,
):
    column_cap, rhs, _ = late_q.shape
    early_copy = pltpu.make_async_copy(early_q, q_ref.at[0, :, pl.ds(0, 2 * rhs)], sems.at[0])
    early_copy.start()
    inv[...] = early_inv[...]
    r_ref[...] = early_r[...]
    lines = lines_ref[...]
    factor(2, [lines[:, rhs * i : rhs * (i + 1)] for i in range(3)], inv, work, upper, r_ref)
    r_copy = pltpu.make_async_copy(r_ref, r_out, sems.at[4])
    r_copy.start()
    part = column_cap // 3
    copies = [
        pltpu.make_async_copy(
            late_q.at[pl.ds(part * i, part)],
            q_ref.at[0, pl.ds(part * i, part), pl.ds(2 * rhs, rhs)],
            sems.at[1 + i],
        )
        for i in range(3)
    ]

    def put(c, block):
        late_q[c] = block
        if (c + 1) % part == 0:
            copies[c // part].start()

    project(2, (v0, v1, v2), inv, put)
    early_copy.wait()
    r_copy.wait()
    for copy in copies:
        copy.wait()


def kernel(
    groups, side, peers_y, rows_total, caps,
    basis_ref, templates_ref, ids_in, live_in, refs_in, lists_in,
    v0, v1, v2, early_q, inv, r_ref, lines_ref, over_ref,
    ids_ref, live_ref, refs_ref, lists_ref, tmpl, ghost1, ghost2, packet1, packet2, layer1, layer2, acc,
    slots_a, slots_b, work, upper,
    load_sem, halo_send, halo_recv, sum_send, sum_recv,
):
    column_cap, rhs, dof = v0.shape[0] - 1, v0.shape[1], v0.shape[2]
    halo_cap = packet1.shape[1]
    zero_own, zero_ghost = column_cap, 8 * halo_cap
    vectors, ghosts, layers = (v0, v1, v2), (ghost1, ghost2), (layer1, layer2)
    packets = (packet1, packet2)
    pieces = side * side
    peers_x = pieces // peers_y
    g = lax.axis_index("group")
    d = lax.axis_index("dom")
    row, col = d // side, d % side
    core, at_y, at_x = d % 2, (d // 2) % peers_y, d // (2 * peers_y)
    me_x = at_x * 2 + core

    def on_z(offset):
        return ((g + offset) % groups, d)

    def on_y(offset):
        return (g, (at_x * peers_y + (at_y + offset) % peers_y) * 2 + core)

    def on_x(offset):
        other = (me_x + offset) % peers_x
        return (g, ((other // 2) * peers_y + at_y) * 2 + other % 2)

    def inside(dx, dy):
        return (row + dx >= 0) & (row + dx < side) & (col + dy >= 0) & (col + dy < side)

    barrier = pltpu.get_barrier_semaphore()

    def greet(device):
        pl.semaphore_signal(barrier, inc=1, device_id=device, device_id_type=MESH)

    expected = 0
    for dx, dy in (DIRECTIONS[k] for k in ORDER):
        target = (g, (row + dx) * side + col + dy)
        pl.when(inside(dx, dy))(functools.partial(greet, target))
        expected += inside(dx, dy).astype(jnp.int32)
    for peers, place in ((groups, on_z), (peers_y, on_y), (peers_x, on_x)):
        for offset in range(1, peers):
            greet(place(offset))
        expected += peers - 1

    loads = [
        pltpu.make_async_copy(source, target, load_sem.at[2 + i])
        for i, (source, target) in enumerate(
            ((lists_in, lists_ref), (live_in, live_ref), (ids_in, ids_ref), (refs_in, refs_ref))
        )
    ]
    for load in loads:
        load.start()
    load_templates = pltpu.make_async_copy(templates_ref, tmpl, load_sem.at[0])
    load_templates.start()
    load_basis = pltpu.make_async_copy(basis_ref.at[0], v0.at[pl.ds(0, column_cap)], load_sem.at[1])
    load_basis.start()

    empty = jnp.zeros((rhs, dof), BF16)
    for vector in vectors:
        vector[zero_own] = empty
    for x in range(2):
        ghosts[x][zero_ghost] = empty
        for k, (dx, dy) in enumerate(DIRECTIONS):
            @pl.when(jnp.logical_not(inside(-dx, -dy)))
            def _():
                ghosts[x][pl.ds(k * halo_cap, halo_cap)] = jnp.zeros((halo_cap, rhs, dof), BF16)

        @pl.when(g == 0)
        def _():
            layers[x][0] = jnp.zeros((column_cap, rhs, dof), BF16)

        @pl.when(g == groups - 1)
        def _():
            layers[x][1] = jnp.zeros((column_cap, rhs, dof), BF16)

    inv[...] = jnp.zeros(inv.shape, F32)
    r_ref[...] = jnp.zeros(r_ref.shape, F32)
    for load in loads:
        load.wait()
    live = live_ref[0]
    load_basis.wait()

    @pl.loop(0, column_cap)
    def _(c):
        v0[c] = v0[c] * (c < live).astype(F32).astype(BF16)

    def plane_copy(x, k):
        dx, dy = DIRECTIONS[k]
        return pltpu.make_async_remote_copy(
            src_ref=packets[x].at[k, pl.ds(0, caps[k])],
            dst_ref=ghosts[x].at[pl.ds(k * halo_cap, caps[k])],
            send_sem=halo_send.at[x, k],
            recv_sem=halo_recv.at[x, k],
            device_id=(g, (row + dx) * side + col + dy),
            device_id_type=MESH,
        )

    def layer_copy(x, up):
        return pltpu.make_async_remote_copy(
            src_ref=vectors[x].at[pl.ds(0, column_cap)],
            dst_ref=layers[x].at[0 if up else 1],
            send_sem=halo_send.at[x, 8 + up],
            recv_sem=halo_recv.at[x, 8 + up],
            device_id=(g + 1 if up else g - 1, d),
            device_id_type=MESH,
        )

    has_up, has_down = g < groups - 1, g > 0

    def pack_packet(x, k):
        for s in range(caps[k]):
            slot = lists_ref[s, 0, k]
            packets[x][k, s] = vectors[x][jnp.where(slot < 0, zero_own, slot)]

    def halo_start(x, packed):
        for k in ORDER:
            if k == 3:
                pl.when(has_up)(lambda: layer_copy(x, 1).start())
                pl.when(has_down)(lambda: layer_copy(x, 0).start())
            if not packed:
                pack_packet(x, k)
            pl.when(inside(*DIRECTIONS[k]))(lambda: plane_copy(x, k).start())

    def layers_wait(x):
        pl.when(has_down)(lambda: layer_copy(x, 1).wait_recv())
        pl.when(has_up)(lambda: layer_copy(x, 0).wait_recv())

    def plane_wait(x):
        for k in ORDER:
            dx, dy = DIRECTIONS[k]
            pl.when(inside(-dx, -dy))(lambda: plane_copy(x, k).wait_recv())

    def halo_sent(x):
        for k in ORDER:
            pl.when(inside(*DIRECTIONS[k]))(lambda: plane_copy(x, k).wait_send())
        pl.when(has_up)(lambda: layer_copy(x, 1).wait_send())
        pl.when(has_down)(lambda: layer_copy(x, 0).wait_send())

    def apply(blocks, c, faces):
        weights = jnp.concatenate([tmpl[ids_ref[f, 0, c]] for f in faces], axis=0)
        return dot(jnp.concatenate(blocks, axis=1), weights)

    def own_pass(x):
        vector = vectors[x]

        @pl.loop(0, column_cap, unroll=UN_OWN)
        def _(c):
            blocks = [vector[c]]
            for q in range(4):
                r = refs_ref[q, c]
                blocks.append(vector[jnp.where((r < 0) | (r >= column_cap), zero_own, r)])
            acc[c] = apply(blocks, c, (0, 3, 4, 5, 6))

    def layer_pass(x):
        @pl.loop(0, column_cap, unroll=UN_LAYER)
        def _(c):
            acc[c] = acc[c] + apply([layers[x][0, c], layers[x][1, c]], c, (1, 2))

    def ghost_pass(x):
        @pl.loop(0, column_cap, unroll=UN_GHOST)
        def _(c):
            blocks = []
            for q in range(4):
                r = refs_ref[q, c]
                blocks.append(ghosts[x][jnp.where(r < column_cap, zero_ghost, r - column_cap)])
            total = acc[c] + apply(blocks, c, (3, 4, 5, 6))
            vectors[x + 1][c] = jnp.where(c < live, total, 0.0).astype(BF16)

    def gram(rows):
        def add(h, carry):
            pair = [
                jnp.concatenate([vectors[i][2 * h], vectors[i][2 * h + 1]], axis=1)
                for i in range(rows[-1] + 1)
            ]
            return tuple(
                total + dot_nt(pair[j], jnp.concatenate(pair[: j + 1], axis=0))
                for j, total in zip(rows, carry)
            )

        start = tuple(jnp.zeros((rhs, rhs * (j + 1)), F32) for j in rows)
        totals = lax.fori_loop(0, column_cap // 2, add, start, unroll=UN_GRAM)
        return [t[:, rhs * i : rhs * (i + 1)] for t in totals for i in range(t.shape[1] // rhs)]

    def mark(blocks):
        spare = [lists_ref[s, 0, k] for k in range(8) for s in range(caps[k], halo_cap)]
        if not spare:
            return blocks
        over = functools.reduce(jnp.maximum, spare) >= 0
        return [jnp.where(over, jnp.nan, blocks[0])] + blocks[1:]

    def pack(block):
        return jnp.concatenate([block[8 * i : 8 * i + 8] for i in range(rhs // 8)], axis=1)

    def unpack(line):
        return jnp.concatenate([line[:, rhs * i : rhs * (i + 1)] for i in range(rhs // 8)], axis=0)

    def send_all(w, hop, peers, place, source, slots, at):
        copies = [
            pltpu.make_async_remote_copy(
                src_ref=source,
                dst_ref=slots.at[at],
                send_sem=sum_send.at[w, hop, offset],
                recv_sem=sum_recv.at[w, hop, offset],
                device_id=place(offset),
                device_id_type=MESH,
            )
            for offset in range(1, peers)
        ]
        for copy in copies:
            copy.start()
        return copies

    def add_up(slots, peers):
        total = slots[0]
        for s in range(1, peers):
            total = total + slots[s]
        return total

    axes_z, axes_y, axes_x = (groups, on_z, g), (peers_y, on_y, at_y), (peers_x, on_x, me_x)

    def reduced(w, blocks):
        routes = ((axes_y, axes_z, axes_x), (axes_z, axes_y, axes_x))
        sums = [
            jnp.concatenate([pack(blocks[0]), pack(blocks[1])], axis=0),
            pack(blocks[2]),
        ]
        sent = []
        for hop in range(3):
            pending = []
            for way, total in enumerate(sums):
                peers, place, at = routes[way][hop]
                slots = (slots_a, slots_b)[way].at[w, hop]
                slots[at] = total
                copies = send_all(2 * w + way, hop, peers, place, slots.at[at], slots, at)
                pending.append((slots, peers, copies))
            yield None
            sums = []
            for slots, peers, copies in pending:
                for copy in copies:
                    copy.wait_recv()
                sent += copies
                sums.append(add_up(slots, peers))
        whole = [sums[0][:8], sums[0][8:], sums[1]]
        yield [unpack(line) * (1.0 / rows_total) for line in whole], sent

    for k in ORDER:
        pack_packet(0, k)
    pl.semaphore_wait(barrier, expected)
    halo_start(0, True)
    load_templates.wait()

    @pl.loop(0, tmpl.shape[0], unroll=4)
    def _(t):
        tmpl[t] = tmpl[t].T

    own_pass(0)
    layers_wait(0)
    layer_pass(0)
    plane_wait(0)
    ghost_pass(0)

    halo_start(1, False)
    early = reduced(0, mark(gram((0, 1))))
    next(early)
    own_pass(1)
    layers_wait(1)
    layer_pass(1)
    next(early)
    plane_wait(1)
    ghost_pass(1)

    late = reduced(1, gram((2,)))
    next(late)
    next(early)
    next(late)
    (first, *second), sent_early = next(early)
    over_ref[0] = jnp.max(jnp.where(first == first, 0, 1))

    def put_at(j):
        def put(c, block):
            early_q[c, rhs * j : rhs * (j + 1), :] = block

        return put

    factor(0, [first], inv, work, upper, r_ref)
    project(0, vectors, inv, put_at(0))
    factor(1, second, inv, work, upper, r_ref)
    next(late)
    project(1, vectors, inv, put_at(1))
    third, sent_late = next(late)
    lines_ref[...] = jnp.concatenate(third, axis=1)
    halo_sent(0)
    halo_sent(1)
    for copy in sent_early + sent_late:
        copy.wait_send()


def solution(mesh):
    groups, pieces = mesh.shape["group"], mesh.shape["dom"]
    side = math.isqrt(pieces)
    peers_y = min(8, pieces // 2)
    peers_x = pieces // peers_y

    def body(basis_start, templates, template_ids, live_columns, face_refs, send_lists):
        _, column_cap, rhs, dof = basis_start.shape
        halo_cap = send_lists.shape[2]
        faces = template_ids.shape[2]
        width = 3 * rhs
        lanes = 128
        rows_total = column_cap * dof * groups * pieces
        vmem, smem = pltpu.VMEM, pltpu.SMEM
        block = (rhs, dof)
        operands = (
            basis_start,
            templates,
            template_ids.transpose(2, 0, 1),
            live_columns,
            face_refs.T,
            send_lists.transpose(2, 0, 1),
        )

        def run(caps, collective_id):
            *early, over = pl.pallas_call(
                functools.partial(kernel, groups, side, peers_y, rows_total, caps),
                out_shape=(
                    vmem((column_cap + 1, *block), BF16),
                    vmem((column_cap + 1, *block), BF16),
                    vmem((column_cap + 1, *block), BF16),
                    vmem((column_cap, 2 * rhs, dof), BF16),
                    vmem((width, lanes), F32),
                    vmem((width, width), F32),
                    vmem((rhs, width), F32),
                    smem((1,), jnp.int32),
                ),
                in_specs=[pl.BlockSpec(memory_space=pltpu.HBM)] * 6,
                out_specs=tuple([pl.BlockSpec(memory_space=vmem)] * 7 + [pl.BlockSpec(memory_space=smem)]),
                scratch_shapes=[
                    smem((faces, 1, column_cap), jnp.int32),
                    smem((1,), jnp.int32),
                    smem((4, column_cap), jnp.int32),
                    smem((halo_cap, 1, 8), jnp.int32),
                    vmem(templates.shape, BF16),
                    vmem((8 * halo_cap + 1, *block), BF16),
                    vmem((8 * halo_cap + 1, *block), BF16),
                    vmem((8, halo_cap, *block), BF16),
                    vmem((8, halo_cap, *block), BF16),
                    vmem((2, column_cap, *block), BF16),
                    vmem((2, column_cap, *block), BF16),
                    vmem((column_cap, *block), F32),
                    vmem((2, 3, 8, 16, lanes), F32),
                    vmem((2, 3, 8, 8, lanes), F32),
                    vmem((rhs, lanes), F32),
                    vmem((rhs, lanes), F32),
                    pltpu.SemaphoreType.DMA((6,)),
                    pltpu.SemaphoreType.DMA((2, 10)),
                    pltpu.SemaphoreType.DMA((2, 10)),
                    pltpu.SemaphoreType.DMA((4, 3, 8)),
                    pltpu.SemaphoreType.DMA((4, 3, 8)),
                ],
                compiler_params=pltpu.CompilerParams(
                    collective_id=collective_id, has_side_effects=True, vmem_limit_bytes=VMEM_MIB * 2**20
                ),
            )(*operands)

            basis_q, r_factor = pl.pallas_call(
                last_kernel,
                out_shape=(
                    jax.ShapeDtypeStruct((1, column_cap, width, dof), BF16),
                    jax.ShapeDtypeStruct((width, width), F32),
                ),
                in_specs=[pl.BlockSpec(memory_space=vmem)] * 7,
                out_specs=(pl.BlockSpec(memory_space=pltpu.HBM), pl.BlockSpec(memory_space=pltpu.HBM)),
                scratch_shapes=[
                    vmem((width, lanes), F32),
                    vmem((rhs, lanes), F32),
                    vmem((rhs, lanes), F32),
                    vmem((column_cap, *block), BF16),
                    vmem((width, width), F32),
                    pltpu.SemaphoreType.DMA((5,)),
                ],
                compiler_params=pltpu.CompilerParams(vmem_limit_bytes=LAST_MIB * 2**20),
            )(*early)
            return basis_q, r_factor, over

        narrow = [halo_cap if 0 in step else CORNER_CAP for step in DIRECTIONS]
        basis_q, r_factor, over = run(narrow, 0)
        return lax.cond(
            over[0] != 0,
            lambda: tuple(run([halo_cap] * 8, 1)[:2]),
            lambda: (basis_q, r_factor),
        )

    return jax.shard_map(
        body,
        mesh=mesh,
        in_specs=(
            P("group", "dom", None, None),
            P(),
            P("group", "dom", None),
            P("dom"),
            P("dom", None),
            P("dom", None, None),
        ),
        out_specs=(P("group", "dom", None, None), P()),
        check_vma=False,
    )
```
